32 devices in a mesh: wide: 8 (over z, y), narrow: 4 (over x, core).
Axes of the slice: x: 2, y: 2, z: 4, core: 2. Of those that a mesh axis runs over, the one named last changes fastest.
Arguments:
- features: bfloat16 [2048, 512], P('wide', 'narrow'), may hold values from -6 to 6
- tile_blocks: bfloat16 [8, 4, 48, 128, 128], P('wide', 'narrow'), may hold values from -0.078125 to 0.078125
- tile_rows: int32 [8, 4, 48], P('wide', 'narrow'), may hold values from 0 to 1
- tile_cols: int32 [8, 4, 48], P('wide', 'narrow'), may hold values from 0 to 3, as said below
- tile_count: int32 [8, 4], P('wide', 'narrow'), may hold values from 12 to 48, as said below
- neighbor_weight: bfloat16 [512, 512], P('narrow'), may hold values from -0.25 to 0.25
- root_weight: bfloat16 [512, 512], P('narrow'), may hold values from -0.25 to 0.25
- output_weight: bfloat16 [512, 512], replicated, may hold values from -0.25 to 0.25
- cotangent: bfloat16 [2048, 512], P('wide'), may hold values from -0.3125 to 0.3125
Outputs:
- layer_output: bfloat16 [2048, 512], P('wide', 'narrow')
- neighbor_grad: float32 [512, 512], P('narrow')
- root_grad: float32 [512, 512], P('narrow')
- output_grad: float32 [512, 512], P(None, 'narrow')
The draws below stay inside these ranges and needn't reach their ends.
Inputs may be any that keep to these rules, and one draw needn't show every extreme that they name: `tile_count`: slots at or past a device's count hold no tiles and are ignored; the largest count is 48 on some device in every draw, the smallest max(1, 12) on another. `tile_cols`: positions may repeat; repeated tiles add. Slot 0 of every device of row block b names the column tile that holds the nodes of row block b + 8 // 2 (counted round).
All inputs are finite; a program needn't handle non-finite values.
Results may differ from the reference program's by a relative error of at most 0.015.
Values may be sent and summed in bfloat16 or wider, within the bound.
A program may use at most 64 MiB of HBM per device.

```python
import jax
import jax.numpy as jnp
from jax import lax

H = 512
TILE = 128
TROWS = 2
TCAP = 48
ROWS = 256
NODES = 2048
QUARTER = 64
COLTILES = 4
N_WIDE = 8
N_NARROW = 4


def draw_tile_count(key, part):
    key = jax.random.fold_in(key, 7)
    first_key, second_key, third_key = jax.random.split(key, 3)
    total = N_WIDE * N_NARROW
    lowest = max(1, TCAP // 4)
    spread = jax.random.randint(first_key, (total,), 0, 17)
    counts = lowest + spread * spread * (TCAP - lowest) // 256
    busiest = jax.random.randint(second_key, (), 0, total)
    quietest = (busiest + 1 + jax.random.randint(third_key, (), 0, total - 1)) % total
    places = jnp.arange(total)
    counts = jnp.where(places == busiest, TCAP, jnp.where(places == quietest, lowest, counts))
    return counts.reshape(N_WIDE, N_NARROW).astype(jnp.int32)


def draw_tile_cols(key, part):
    key = jax.random.fold_in(key, 11)
    columns = jax.random.randint(key, (N_WIDE, N_NARROW, TCAP), 0, COLTILES)
    across = (jnp.arange(N_WIDE, dtype=jnp.int32) + N_WIDE // 2) % N_WIDE
    holding = across * QUARTER // TILE
    columns = columns.at[:, :, 0].set(jnp.broadcast_to(holding[:, None], (N_WIDE, N_NARROW)))
    return columns.astype(jnp.int32)


def touch_ends(entries, rng, least, high):
    index_at = [jax.random.randint(jax.random.fold_in(rng, axis), (), 0, length) for axis, length in enumerate(entries.shape)]
    main_axis = entries.shape.index(max(entries.shape))
    beside = index_at[:main_axis] + [(index_at[main_axis] + 1) % entries.shape[main_axis]] + index_at[main_axis + 1:]
    return entries.at[tuple(index_at)].set(least).at[tuple(beside)].set(high)


def levels(key, extent, cuts, smallest, largest):
    gain = 1.0
    for position, blocks in cuts:
        draws = jax.random.uniform(jax.random.fold_in(jax.random.fold_in(key, 6), position), (blocks,), jnp.float32, smallest / len(cuts), largest / len(cuts))
        gain = gain * jnp.repeat(jnp.exp(draws), extent[position] // blocks).reshape((-1,) + (1,) * (len(extent) - 1 - position))
    return gain


def centred(own_key, shape, scale, bound, cuts=(), kind=jnp.bfloat16):
    entries = scale * jax.random.normal(own_key, shape, jnp.float32)
    if cuts:
        entries = entries * levels(own_key, shape, cuts, -0.22, 0.18)
    return jnp.clip(entries, -bound, bound).astype(kind)


def setup_inputs(seed: int = 0) -> dict:
    keys = jax.random.split(jax.random.key(seed), 10)
    return {
        "features": centred(keys[0], (NODES, H), 1.0, 6.0, ((0, 8), (1, 4))),
        "tile_blocks": centred(keys[1], (N_WIDE, N_NARROW, TCAP, TILE, TILE), (256 * TCAP // TROWS) ** -0.5, 0.078125, ((0, 8), (1, 4))),
        "tile_rows": touch_ends(jax.random.randint(keys[2], (N_WIDE, N_NARROW, TCAP), 0, TROWS), jax.random.fold_in(keys[2], 1), 0, TROWS - 1).astype(jnp.int32),
        "tile_cols": draw_tile_cols(jax.random.fold_in(keys[9], 71), 0),
        "tile_count": draw_tile_count(jax.random.fold_in(keys[9], 71), 0),
        "neighbor_weight": centred(keys[5], (H, H), H ** -0.5, 0.25, ((0, 4),)),
        "root_weight": centred(keys[6], (H, H), H ** -0.5, 0.25, ((0, 4),)),
        "output_weight": centred(keys[7], (H, H), H ** -0.5, 0.25),
        "cotangent": centred(keys[8], (NODES, H), (NODES ** -0.5), 0.3125, ((0, 8),)),
    }


def aggregate(features, tile_blocks, tile_rows, tile_cols, tile_count):
    groups = features.reshape(N_WIDE, N_NARROW, QUARTER, H).transpose(1, 0, 2, 3)
    groups = groups.reshape(N_NARROW, COLTILES, TILE, H)
    slot_ids = jnp.arange(TCAP, dtype=jnp.int32)
    group_ids = jnp.arange(N_NARROW, dtype=jnp.int32)
    row_ids = jnp.arange(TROWS, dtype=jnp.int32)

    def one_block(inputs):
        block_tiles, block_rows, block_cols, block_count = inputs
        alive = (slot_ids[None, :] < block_count[:, None]).astype(jnp.float32)
        picked = groups[group_ids[:, None], block_cols]
        product = jnp.einsum("gtij,gtjh->gtih", block_tiles.astype(jnp.float32), picked.astype(jnp.float32))
        placing = alive[:, :, None] * (block_rows[:, :, None] == row_ids[None, None, :]).astype(jnp.float32)
        return jnp.einsum("gtr,gtih->rih", placing, product).reshape(ROWS, H)

    summed = lax.map(one_block, (tile_blocks, tile_rows, tile_cols, tile_count))
    return summed.reshape(NODES, H).astype(jnp.bfloat16)


def reference(features, tile_blocks, tile_rows, tile_cols, tile_count, neighbor_weight, root_weight, output_weight, cotangent):
    agg = aggregate(features, tile_blocks, tile_rows, tile_cols, tile_count)
    pre = jnp.dot(agg, neighbor_weight, preferred_element_type=jnp.float32) + jnp.dot(features, root_weight, preferred_element_type=jnp.float32)
    hidden = jax.nn.silu(pre).astype(jnp.bfloat16)
    layer_output = (features.astype(jnp.float32) + jnp.dot(hidden, output_weight, preferred_element_type=jnp.float32)).astype(jnp.bfloat16)
    hidden_grad = jnp.dot(cotangent, output_weight.T, preferred_element_type=jnp.float32)
    sigmoid_pre = jax.nn.sigmoid(pre)
    pre_grad = (hidden_grad * sigmoid_pre * (1.0 + pre * (1.0 - sigmoid_pre))).astype(jnp.bfloat16)
    neighbor_grad = jnp.dot(agg.T, pre_grad, preferred_element_type=jnp.float32)
    root_grad = jnp.dot(features.T, pre_grad, preferred_element_type=jnp.float32)
    output_grad = jnp.dot(hidden.T, cotangent, preferred_element_type=jnp.float32)
    return layer_output, neighbor_grad, root_grad, output_grad
```

```python
import functools
import math

import jax
import jax.numpy as jnp
from jax import lax
from jax.experimental import pallas as pl
from jax.experimental.pallas import tpu as pltpu
from jax.sharding import PartitionSpec as P


def tile_sum(block_tiles, row_ids, col_ids, live_count, column_tiles, tile_rows_count):
    capacity = block_tiles.shape[0]
    block_size = math.gcd(capacity, 24)
    tile_side = block_tiles.shape[-1]
    feature_width = column_tiles.shape[-1]
    row_range = jnp.arange(tile_rows_count, dtype=jnp.int32)
    slot_range = jnp.arange(block_size, dtype=jnp.int32)

    def one_turn(turn_index, running):
        first_slot = turn_index * block_size
        some_tiles = lax.dynamic_slice_in_dim(block_tiles, first_slot, block_size, 0)
        some_rows = lax.dynamic_slice_in_dim(row_ids, first_slot, block_size, 0)
        some_cols = lax.dynamic_slice_in_dim(col_ids, first_slot, block_size, 0)
        picked = column_tiles[some_cols]
        product = jnp.einsum("tij,tjh->tih", some_tiles, picked, preferred_element_type=jnp.float32)
        alive = (first_slot + slot_range < live_count).astype(jnp.float32)
        placing = alive[:, None] * (some_rows[:, None] == row_range[None, :]).astype(jnp.float32)
        return running + jnp.einsum("tr,tih->rih", placing, product)

    block_turns = (live_count + block_size - 1) // block_size
    start_value = jnp.zeros((tile_rows_count, tile_side, feature_width), jnp.float32)
    summed = lax.fori_loop(0, block_turns, one_turn, start_value)
    return summed.reshape(tile_rows_count * tile_side, feature_width)


def per_device_large(
    features,
    tile_blocks,
    tile_rows,
    tile_cols,
    tile_count,
    neighbor_weight,
    root_weight,
    output_weight,
    cotangent,
):
    node_rows = features.shape[0]
    slice_width = features.shape[1]
    wide_count = lax.axis_size("wide")
    narrow_count = lax.axis_size("narrow")
    tile_side = tile_blocks.shape[-1]
    tile_rows_count = node_rows // tile_side
    group_rows = node_rows // narrow_count
    all_tiles, all_rows, all_cols, all_counts = (
        lax.all_gather(tile_blocks, "narrow", axis=1, tiled=True),
        lax.all_gather(tile_rows, "narrow", axis=1, tiled=True),
        lax.all_gather(tile_cols, "narrow", axis=1, tiled=True),
        lax.all_gather(tile_count, "narrow", axis=1, tiled=True),
    )
    columns = lax.all_gather(features, "wide", axis=0, tiled=True)
    groups = columns.reshape(wide_count, narrow_count, group_rows, slice_width).transpose(
        1, 0, 2, 3
    )
    groups = groups.reshape(narrow_count, -1, tile_side, slice_width)
    running = jnp.zeros((node_rows, slice_width), jnp.float32)
    for source in range(narrow_count):
        running = running + tile_sum(
            all_tiles[0, source],
            all_rows[0, source],
            all_cols[0, source],
            all_counts[0, source],
            groups[source],
            tile_rows_count,
        )
    agg = running.astype(jnp.bfloat16)
    partial_pre = jnp.dot(agg, neighbor_weight, preferred_element_type=jnp.float32) + jnp.dot(
        features, root_weight, preferred_element_type=jnp.float32
    )
    pre = lax.psum(partial_pre, "narrow")
    hidden = jax.nn.silu(pre).astype(jnp.bfloat16)
    narrow_index = lax.axis_index("narrow")
    out_columns = lax.dynamic_slice_in_dim(
        output_weight, narrow_index * slice_width, slice_width, 1
    )
    layer_output = (
        features.astype(jnp.float32)
        + jnp.dot(hidden, out_columns, preferred_element_type=jnp.float32)
    ).astype(jnp.bfloat16)
    hidden_grad = jnp.dot(cotangent, output_weight.T, preferred_element_type=jnp.float32)
    sigmoid_pre = jax.nn.sigmoid(pre)
    pre_grad = (hidden_grad * sigmoid_pre * (1.0 + pre * (1.0 - sigmoid_pre))).astype(jnp.bfloat16)
    cot_columns = lax.dynamic_slice_in_dim(cotangent, narrow_index * slice_width, slice_width, 1)
    neighbor_part = jnp.dot(agg.T, pre_grad, preferred_element_type=jnp.float32)
    root_part = jnp.dot(features.T, pre_grad, preferred_element_type=jnp.float32)
    output_part = jnp.dot(hidden.T, cot_columns, preferred_element_type=jnp.float32)
    neighbor_grad, root_grad, output_grad = lax.psum(
        (neighbor_part, root_part, output_part), "wide"
    )
    return (layer_output, neighbor_grad, root_grad, output_grad)


Y_SIZE = 2
CORES = 2
MESH = pl.DeviceIdType.MESH


def fused_kernel(
    wide, narrow,
    x_hbm, t_hbm, rows_ref, cols_ref, count_ref, wn_hbm, wr_hbm, ow_hbm, cot_hbm,
    grads_out, lo_out,
    x_vm, tiles, ow, cot, fg, weights, dense, part, part_bf, agg_in, agg_r, agg_cols,
    pg, hid, grad32, grad, from_y, to_z, from_z, gall, lo,
    local_sem, send_sem, recv_sem,
):
    z_size = wide // Y_SIZE
    me_b = lax.axis_index("wide")
    me_n = lax.axis_index("narrow")
    z, y = me_b // Y_SIZE, me_b % Y_SIZE
    other_y = 1 - y
    core_n = me_n // CORES * CORES + (1 - me_n % CORES)
    x_n = (me_n + CORES) % narrow
    xc_n = (core_n + CORES) % narrow
    node_rows = x_hbm.shape[0]
    width = x_hbm.shape[1]
    hidden_width = ow_hbm.shape[0]
    group = node_rows // narrow
    side = t_hbm.shape[-1]
    slots = t_hbm.shape[2]
    piece = gall.shape[1]
    f32, bf16 = jnp.float32, jnp.bfloat16
    y_dev = (z * Y_SIZE + other_y, me_n)

    def group_rows(n):
        return pl.ds(pl.multiple_of(n * group, group), group)

    def slice_cols(n):
        return pl.ds(pl.multiple_of(n * width, width), width)

    def z_dev(dz):
        return (lax.rem(z + dz, z_size) * Y_SIZE + y, me_n)

    used = [0]
    pending = []

    def send(src, dst, device):
        k = used[0]
        used[0] += 1
        copy = pltpu.make_async_remote_copy(
            src_ref=src, dst_ref=dst, send_sem=send_sem.at[k], recv_sem=recv_sem.at[k],
            device_id=device, device_id_type=MESH,
        )
        copy.start()
        pending.append(copy)
        return copy

    own_x = pltpu.make_async_copy(
        x_hbm.at[group_rows(me_n), :], fg.at[me_b, :, slice_cols(me_n)], local_sem.at[0]
    )
    own_wn = pltpu.make_async_copy(wn_hbm, weights.at[0, slice_cols(me_n), :], local_sem.at[1])
    own_wr = pltpu.make_async_copy(wr_hbm, weights.at[1, slice_cols(me_n), :], local_sem.at[2])
    tile_copy = pltpu.make_async_copy(t_hbm.at[0, 0], tiles, local_sem.at[3])
    ow_copy = pltpu.make_async_copy(ow_hbm, ow, local_sem.at[4])
    cot_copy = pltpu.make_async_copy(cot_hbm, cot, local_sem.at[5])
    x_copy = pltpu.make_async_copy(x_hbm, x_vm, local_sem.at[6])
    for copy in (own_x, tile_copy, cot_copy, ow_copy, own_wn, own_wr, x_copy):
        copy.start()

    barrier = pltpu.get_barrier_semaphore()
    partners = [(me_b, n) for n in (core_n, x_n, xc_n)]
    partners += [z_dev(dz) for dz in range(1, z_size)] + [y_dev]
    for device in partners:
        pl.semaphore_signal(barrier, inc=1, device_id=device, device_id_type=MESH)
    pl.semaphore_wait(barrier, len(partners))

    narrow_partners = (xc_n, x_n, core_n)
    first = [
        send(x_hbm.at[group_rows(n), :], fg.at[me_b, :, slice_cols(me_n)], (me_b, n))
        for n in narrow_partners
    ]
    own_x.wait()
    for copy in first:
        copy.wait_recv()
    z_order = sorted(range(1, z_size), key=lambda dz: abs(dz - z_size / 2))
    blocks = {dz: send(fg.at[me_b], fg.at[me_b], z_dev(dz)) for dz in z_order}
    from_y_blocks = [send(fg.at[me_b], fg.at[me_b], y_dev)]
    w_core = [
        send(w, weights.at[i, slice_cols(me_n), :], (me_b, core_n))
        for i, w in enumerate((wn_hbm, wr_hbm))
    ]
    w_x = [
        send(w, weights.at[i, slice_cols(me_n), :], (me_b, x_n))
        for i, w in enumerate((wn_hbm, wr_hbm))
    ]

    tile_copy.wait()
    live = count_ref[0, 0]
    chunk = 32
    positions = dense.shape[0] // side * (dense.shape[1] // side)
    across = dense.shape[1] // side

    def densify(step, _):
        at = pl.ds(pl.multiple_of(step * chunk, chunk), chunk)

        def add_slot(s, sums):
            tile = tiles[s, at, :].astype(f32)
            place = rows_ref[0, 0, s] * across + cols_ref[0, 0, s]
            place = jnp.where(s < live, place, -1)
            return tuple(
                sums[p] + tile * jnp.where(place == p, 1.0, 0.0).astype(f32)
                for p in range(positions)
            )

        sums = lax.fori_loop(
            0, slots, add_slot, tuple(jnp.zeros((chunk, side), f32) for _ in range(positions))
        )
        for p in range(positions):
            row = pl.ds(pl.multiple_of(p // across * side + step * chunk, chunk), chunk)
            dense[row, pl.ds(p % across * side, side)] = sums[p].astype(bf16)
        return 0

    lax.fori_loop(0, side // chunk, densify, 0)

    for dz in z_order:
        blocks[dz].wait_recv()
        b = lax.rem(z + z_size - dz, z_size) * Y_SIZE + y
        from_y_blocks.append(send(fg.at[b], fg.at[b], y_dev))
    w_fwd = []
    for i in range(2):
        w_x[i].wait_recv()
        w_fwd.append(
            send(
                weights.at[i, slice_cols(x_n), :], weights.at[i, slice_cols(x_n), :],
                (me_b, core_n),
            )
        )
    cot_copy.wait()
    ow_copy.wait()
    hidden_grad = lax.dot_general(
        cot[group_rows(me_n), :], ow[...], (((1,), (1,)), ((), ())), preferred_element_type=f32
    )
    for copy in from_y_blocks:
        copy.wait_recv()
    part[...] = jnp.dot(
        dense[...], fg[...].reshape(wide * group, hidden_width), preferred_element_type=f32
    )
    part_bf[...] = part[...].astype(bf16)
    arriving = [
        send(part_bf.at[group_rows(n), :], agg_in.at[i], (me_b, n))
        for i, n in enumerate(narrow_partners)
    ]
    own_wn.wait()
    own_wr.wait()
    for copy in w_core + w_fwd:
        copy.wait_recv()
    pre = jnp.dot(fg[me_b], weights[1], preferred_element_type=f32)
    agg32 = part[group_rows(me_n), :]
    for i, copy in enumerate(arriving):
        copy.wait_recv()
        agg32 = agg32 + agg_in[i].astype(f32)
    agg_r[...] = agg32.astype(bf16)
    agg_moves = [
        send(agg_r.at[:, slice_cols(n)], agg_cols.at[group_rows(me_n), :], (me_b, n))
        for n in narrow_partners
    ]
    pre = pre + jnp.dot(agg_r[...], weights[0], preferred_element_type=f32)
    sig = jax.nn.sigmoid(pre)
    mine = group_rows(me_n)
    pg[mine, :] = (hidden_grad * sig * (1.0 + pre * (1.0 - sig))).astype(bf16)
    hid[mine, :] = (pre * sig).astype(bf16)
    pg_x = send(pg.at[mine, :], pg.at[mine, :], (me_b, x_n))
    hid_x = send(hid.at[mine, :], hid.at[mine, :], (me_b, x_n))
    pg_core = [send(pg.at[mine, :], pg.at[mine, :], (me_b, core_n))]
    hid_core = [send(hid.at[mine, :], hid.at[mine, :], (me_b, core_n))]
    agg_cols[mine, :] = agg_r[:, slice_cols(me_n)]
    theirs = group_rows(x_n)
    pg_x.wait_recv()
    pg_core.append(send(pg.at[theirs, :], pg.at[theirs, :], (me_b, core_n)))
    hid_x.wait_recv()
    hid_core.append(send(hid.at[theirs, :], hid.at[theirs, :], (me_b, core_n)))

    x_copy.wait()
    for copy in agg_moves + pg_core:
        copy.wait_recv()
    contract_rows = (((0,), (0,)), ((), ()))
    grad32[pl.ds(0, width), :] = lax.dot_general(
        agg_cols[...], pg[...], contract_rows, preferred_element_type=f32
    )
    grad32[pl.ds(width, width), :] = lax.dot_general(
        x_vm[...], pg[...], contract_rows, preferred_element_type=f32
    )
    for copy in hid_core:
        copy.wait_recv()
    grad32[pl.ds(2 * width, width), :] = lax.dot_general(
        cot[:, slice_cols(me_n)], hid[...], contract_rows, preferred_element_type=f32
    )
    grad[...] = grad32[...].astype(bf16)

    def piece_rows(b):
        return pl.ds(pl.multiple_of(b * piece, 16), piece)

    def z_at(dz):
        return lax.rem(z + dz, z_size)

    halves = [
        send(grad.at[piece_rows(z_at(dz) * Y_SIZE + other_y), :], from_y.at[dz], y_dev)
        for dz in z_order + [0]
    ]
    arriving_z = []
    for dz, copy in zip(z_order + [0], halves):
        copy.wait_recv()
        both = grad32[piece_rows(z_at(dz) * Y_SIZE + y), :] + from_y[dz].astype(f32)
        if dz:
            to_z[dz] = both.astype(bf16)
            arriving_z.append((dz, send(to_z.at[dz], from_z.at[dz], z_dev(dz))))
    lo[...] = jnp.dot(hid[...], ow[:, slice_cols(me_n)], preferred_element_type=f32)
    lo_copy = pltpu.make_async_copy(lo, lo_out, local_sem.at[7])
    lo_copy.start()
    for dz, copy in arriving_z:
        copy.wait_recv()
        both = both + from_z[dz].astype(f32)
    gall[me_b] = both.astype(bf16)
    done = {dz: send(gall.at[me_b], gall.at[me_b], z_dev(dz)) for dz in z_order}
    last = [send(gall.at[me_b], gall.at[me_b], y_dev)]
    for dz in z_order:
        done[dz].wait_recv()
        b = lax.rem(z + z_size - dz, z_size) * Y_SIZE + y
        last.append(send(gall.at[b], gall.at[b], y_dev))
    for copy in last:
        copy.wait_recv()
    out_copy = pltpu.make_async_copy(gall, grads_out, local_sem.at[8])
    out_copy.start()
    for copy in pending:
        copy.wait_send()
    lo_copy.wait()
    out_copy.wait()


def per_device_fused(
    wide, narrow,
    features, tile_blocks, tile_rows, tile_cols, tile_count,
    neighbor_weight, root_weight, output_weight, cotangent,
):
    node_rows, width = features.shape
    hidden_width = output_weight.shape[0]
    group = node_rows // narrow
    side = tile_blocks.shape[-1]
    z_size = wide // Y_SIZE
    piece = 3 * width // wide
    bf16, f32 = jnp.bfloat16, jnp.float32
    copies = 11 + 3 * (z_size + z_size) + 12 + z_size + 3
    hbm = pl.BlockSpec(memory_space=pl.ANY)
    smem = pl.BlockSpec(memory_space=pltpu.SMEM)
    grads, product = pl.pallas_call(
        functools.partial(fused_kernel, wide, narrow),
        out_shape=(
            jax.ShapeDtypeStruct((wide, piece, hidden_width), bf16),
            jax.ShapeDtypeStruct((node_rows, width), f32),
        ),
        in_specs=[hbm, hbm, smem, smem, smem, hbm, hbm, hbm, hbm],
        out_specs=(hbm, hbm),
        scratch_shapes=[
            pltpu.VMEM((node_rows, width), bf16),
            pltpu.VMEM(tile_blocks.shape[2:], bf16),
            pltpu.VMEM((hidden_width, hidden_width), bf16),
            pltpu.VMEM((node_rows, hidden_width), bf16),
            pltpu.VMEM((wide, group, hidden_width), bf16),
            pltpu.VMEM((2, hidden_width, hidden_width), bf16),
            pltpu.VMEM((node_rows, wide * group), bf16),
            pltpu.VMEM((node_rows, hidden_width), f32),
            pltpu.VMEM((node_rows, hidden_width), bf16),
            pltpu.VMEM((narrow - 1, group, hidden_width), bf16),
            pltpu.VMEM((group, hidden_width), bf16),
            pltpu.VMEM((node_rows, width), bf16),
            pltpu.VMEM((node_rows, hidden_width), bf16),
            pltpu.VMEM((node_rows, hidden_width), bf16),
            pltpu.VMEM((3 * width, hidden_width), f32),
            pltpu.VMEM((3 * width, hidden_width), bf16),
            pltpu.VMEM((z_size, piece, hidden_width), bf16),
            pltpu.VMEM((z_size, piece, hidden_width), bf16),
            pltpu.VMEM((z_size, piece, hidden_width), bf16),
            pltpu.VMEM((wide, piece, hidden_width), bf16),
            pltpu.VMEM((node_rows, width), f32),
            pltpu.SemaphoreType.DMA((9,)),
            pltpu.SemaphoreType.DMA((copies,)),
            pltpu.SemaphoreType.DMA((copies,)),
        ],
        compiler_params=pltpu.CompilerParams(
            collective_id=0, has_side_effects=True, vmem_limit_bytes=40 * 1024 * 1024
        ),
    )(
        features, tile_blocks, tile_rows, tile_cols, tile_count,
        neighbor_weight, root_weight, output_weight, cotangent,
    )
    grads = grads.reshape(3 * width, hidden_width)
    layer_output = (features.astype(f32) + product).astype(bf16)
    return (
        layer_output,
        grads[:width].astype(f32),
        grads[width : 2 * width].astype(f32),
        grads[2 * width :].T.astype(f32),
    )


def solution(mesh):
    wide, narrow = mesh.shape["wide"], mesh.shape["narrow"]
    if wide == 8 and narrow == 4:
        per_device = functools.partial(per_device_fused, wide, narrow)
    else:
        per_device = per_device_large
    return jax.shard_map(
        per_device,
        mesh=mesh,
        in_specs=(
            P("wide", "narrow"),
            P("wide", "narrow", None, None, None),
            P("wide", "narrow", None),
            P("wide", "narrow", None),
            P("wide", "narrow"),
            P("narrow", None),
            P("narrow", None),
            P(),
            P("wide", None),
        ),
        out_specs=(P("wide", "narrow"), P("narrow", None), P("narrow", None), P(None, "narrow")),
        check_vma=False,
    )
```

```python
import functools
import math

import jax
import jax.numpy as jnp
from jax import lax
from jax.experimental import pallas as pl
from jax.experimental.pallas import tpu as pltpu
from jax.sharding import PartitionSpec as P


def tile_sum(block_tiles, row_ids, col_ids, live_count, column_tiles, tile_rows_count):
    capacity = block_tiles.shape[0]
    block_size = math.gcd(capacity, 24)
    tile_side = block_tiles.shape[-1]
    feature_width = column_tiles.shape[-1]
    row_range = jnp.arange(tile_rows_count, dtype=jnp.int32)
    slot_range = jnp.arange(block_size, dtype=jnp.int32)

    def one_turn(turn_index, running):
        first_slot = turn_index * block_size
        some_tiles = lax.dynamic_slice_in_dim(block_tiles, first_slot, block_size, 0)
        some_rows = lax.dynamic_slice_in_dim(row_ids, first_slot, block_size, 0)
        some_cols = lax.dynamic_slice_in_dim(col_ids, first_slot, block_size, 0)
        picked = column_tiles[some_cols]
        product = jnp.einsum("tij,tjh->tih", some_tiles, picked, preferred_element_type=jnp.float32)
        alive = (first_slot + slot_range < live_count).astype(jnp.float32)
        placing = alive[:, None] * (some_rows[:, None] == row_range[None, :]).astype(jnp.float32)
        return running + jnp.einsum("tr,tih->rih", placing, product)

    block_turns = (live_count + block_size - 1) // block_size
    start_value = jnp.zeros((tile_rows_count, tile_side, feature_width), jnp.float32)
    summed = lax.fori_loop(0, block_turns, one_turn, start_value)
    return summed.reshape(tile_rows_count * tile_side, feature_width)


def per_device_large(
    features,
    tile_blocks,
    tile_rows,
    tile_cols,
    tile_count,
    neighbor_weight,
    root_weight,
    output_weight,
    cotangent,
):
    node_rows = features.shape[0]
    slice_width = features.shape[1]
    wide_count = lax.axis_size("wide")
    narrow_count = lax.axis_size("narrow")
    tile_side = tile_blocks.shape[-1]
    tile_rows_count = node_rows // tile_side
    group_rows = node_rows // narrow_count
    all_tiles, all_rows, all_cols, all_counts = (
        lax.all_gather(tile_blocks, "narrow", axis=1, tiled=True),
        lax.all_gather(tile_rows, "narrow", axis=1, tiled=True),
        lax.all_gather(tile_cols, "narrow", axis=1, tiled=True),
        lax.all_gather(tile_count, "narrow", axis=1, tiled=True),
    )
    columns = lax.all_gather(features, "wide", axis=0, tiled=True)
    groups = columns.reshape(wide_count, narrow_count, group_rows, slice_width).transpose(
        1, 0, 2, 3
    )
    groups = groups.reshape(narrow_count, -1, tile_side, slice_width)
    running = jnp.zeros((node_rows, slice_width), jnp.float32)
    for source in range(narrow_count):
        running = running + tile_sum(
            all_tiles[0, source],
            all_rows[0, source],
            all_cols[0, source],
            all_counts[0, source],
            groups[source],
            tile_rows_count,
        )
    agg = running.astype(jnp.bfloat16)
    partial_pre = jnp.dot(agg, neighbor_weight, preferred_element_type=jnp.float32) + jnp.dot(
        features, root_weight, preferred_element_type=jnp.float32
    )
    pre = lax.psum(partial_pre, "narrow")
    hidden = jax.nn.silu(pre).astype(jnp.bfloat16)
    narrow_index = lax.axis_index("narrow")
    out_columns = lax.dynamic_slice_in_dim(
        output_weight, narrow_index * slice_width, slice_width, 1
    )
    layer_output = (
        features.astype(jnp.float32)
        + jnp.dot(hidden, out_columns, preferred_element_type=jnp.float32)
    ).astype(jnp.bfloat16)
    hidden_grad = jnp.dot(cotangent, output_weight.T, preferred_element_type=jnp.float32)
    sigmoid_pre = jax.nn.sigmoid(pre)
    pre_grad = (hidden_grad * sigmoid_pre * (1.0 + pre * (1.0 - sigmoid_pre))).astype(jnp.bfloat16)
    cot_columns = lax.dynamic_slice_in_dim(cotangent, narrow_index * slice_width, slice_width, 1)
    neighbor_part = jnp.dot(agg.T, pre_grad, preferred_element_type=jnp.float32)
    root_part = jnp.dot(features.T, pre_grad, preferred_element_type=jnp.float32)
    output_part = jnp.dot(hidden.T, cot_columns, preferred_element_type=jnp.float32)
    neighbor_grad, root_grad, output_grad = lax.psum(
        (neighbor_part, root_part, output_part), "wide"
    )
    return (layer_output, neighbor_grad, root_grad, output_grad)


Y_SIZE = 2
CORES = 2
MESH = pl.DeviceIdType.MESH


def fused_kernel(
    wide, narrow,
    x_hbm, t_hbm, rows_ref, cols_ref, count_ref, wn_hbm, wr_hbm, ow_hbm, cot_hbm,
    grads_out, lo_out,
    xf, tiles, ow, cot, wn, wr, dense, part, part_bf, pre_in, agg,
    pg, hid, grad32, grad, from_y, to_z, from_z, gall, lo,
    local_sem, send_sem, recv_sem,
):
    z_size = wide // Y_SIZE
    me_b = lax.axis_index("wide")
    me_n = lax.axis_index("narrow")
    z, y = me_b // Y_SIZE, me_b % Y_SIZE
    other_y = 1 - y
    core_n = me_n // CORES * CORES + (1 - me_n % CORES)
    x_n = (me_n + CORES) % narrow
    xc_n = (core_n + CORES) % narrow
    node_rows, width = x_hbm.shape
    hidden_width = ow_hbm.shape[0]
    group = node_rows // narrow
    side = t_hbm.shape[-1]
    slots = t_hbm.shape[2]
    piece = width // wide
    tile_rows_count = node_rows // side
    across = dense.shape[-1] // side
    f32, bf16 = jnp.float32, jnp.bfloat16
    y_dev = (z * Y_SIZE + other_y, me_n)

    def group_rows(n):
        return pl.ds(pl.multiple_of(n * group, group), group)

    def slice_cols(n):
        return pl.ds(pl.multiple_of(n * width, width), width)

    def z_at(dz):
        return lax.rem(z + dz, z_size)

    def z_dev(dz):
        return (z_at(dz) * Y_SIZE + y, me_n)

    def z_source(dz):
        return lax.rem(z + z_size - dz, z_size) * Y_SIZE + y

    used = [0]
    pending = []

    def send(src, dst, device):
        k = used[0]
        used[0] += 1
        copy = pltpu.make_async_remote_copy(
            src_ref=src, dst_ref=dst, send_sem=send_sem.at[k], recv_sem=recv_sem.at[k],
            device_id=device, device_id_type=MESH,
        )
        copy.start()
        pending.append(copy)
        return copy

    barrier = pltpu.get_barrier_semaphore()
    partners = [(me_b, n) for n in (core_n, x_n, xc_n)]
    partners += [z_dev(dz) for dz in range(1, z_size)] + [y_dev]
    for device in partners:
        pl.semaphore_signal(barrier, inc=1, device_id=device, device_id_type=MESH)

    local = [
        pltpu.make_async_copy(src, dst, local_sem.at[k])
        for k, (src, dst) in enumerate(
            (
                (t_hbm.at[0, 0], tiles),
                (x_hbm, xf.at[me_b]),
                (wr_hbm, wr),
                (wn_hbm, wn),
                (cot_hbm, cot),
                (ow_hbm, ow),
            )
        )
    ]
    for copy in local:
        copy.start()
    tile_copy, x_copy, wr_copy, wn_copy, cot_copy, ow_copy = local

    live = count_ref[0, 0]
    chunk = 32
    positions = tile_rows_count * across
    steps = side // chunk

    def densify(step, _):
        at = pl.ds(pl.multiple_of(step * chunk, chunk), chunk)

        def add_slot(s, sums):
            tile = tiles[s, at, :].astype(f32)
            place = rows_ref[0, 0, s] * across + cols_ref[0, 0, s]
            place = jnp.where(s < live, place, -1)
            return tuple(
                sums[p] + tile * jnp.where(place == p, 1.0, 0.0).astype(f32)
                for p in range(positions)
            )

        sums = lax.fori_loop(
            0, slots, add_slot, tuple(jnp.zeros((chunk, side), f32) for _ in range(positions))
        )
        for p in range(positions):
            dense[me_n, p // across, at, pl.ds(p % across * side, side)] = sums[p].astype(bf16)
        return 0

    def half(n, h):
        return dense.at[n, :, pl.ds(h * (side // 2), side // 2), :]

    tile_copy.wait()
    lax.fori_loop(0, steps // 2, densify, 0)
    pl.semaphore_wait(barrier, len(partners))

    z_order = sorted(range(1, z_size), key=lambda dz: abs(dz - z_size / 2))
    blocks = {dz: send(x_hbm, xf.at[me_b], z_dev(dz)) for dz in z_order}
    y_blocks = [send(x_hbm, xf.at[me_b], y_dev)]
    dense_x = [send(half(me_n, 0), half(me_n, 0), (me_b, x_n))]
    dense_core = [send(half(me_n, 0), half(me_n, 0), (me_b, core_n))]
    lax.fori_loop(steps // 2, steps, densify, 0)
    dense_x.append(send(half(me_n, 1), half(me_n, 1), (me_b, x_n)))
    dense_core.append(send(half(me_n, 1), half(me_n, 1), (me_b, core_n)))
    dense_fwd = []

    def pass_block(dz):
        blocks[dz].wait_recv()
        b = z_source(dz)
        y_blocks.append(send(xf.at[b], xf.at[b], y_dev))

    def pass_half(h):
        dense_x[h].wait_recv()
        dense_fwd.append(send(half(x_n, h), half(x_n, h), (me_b, core_n)))

    for dz in z_order[1:]:
        pass_block(dz)
    pass_half(0)
    pass_block(z_order[0])
    cot_copy.wait()
    ow_copy.wait()
    hidden_grad = lax.dot_general(
        cot[group_rows(me_n), :], ow[...], (((1,), (1,)), ((), ())), preferred_element_type=f32
    )
    pass_half(1)
    x_copy.wait()
    wr_copy.wait()
    wn_copy.wait()
    part[...] = jnp.dot(xf[me_b], wr[...], preferred_element_type=f32)

    for copy in y_blocks:
        copy.wait_recv()

    def product(n):
        column_tiles = xf[:, group_rows(n), :].reshape(wide * group, width)
        return jnp.dot(
            dense[n].reshape(node_rows, wide * group), column_tiles, preferred_element_type=f32
        )

    total = product(me_n)
    for copy in dense_core:
        copy.wait_recv()
    total = total + product(core_n)
    total = total + product(x_n)
    for copy in dense_fwd:
        copy.wait_recv()
    total = total + product(xc_n)
    agg[...] = total.astype(bf16)

    arriving = []
    narrow_partners = (xc_n, x_n, core_n)
    for i, n in enumerate(narrow_partners):
        at = group_rows(n)
        there = part[at, :] + jnp.dot(agg[at, :], wn[...], preferred_element_type=f32)
        part_bf[i] = there.astype(bf16)
        arriving.append(send(part_bf.at[i], pre_in.at[i], (me_b, n)))
    mine = group_rows(me_n)
    pre = part[mine, :] + jnp.dot(agg[mine, :], wn[...], preferred_element_type=f32)
    for i, copy in enumerate(arriving):
        copy.wait_recv()
        pre = pre + pre_in[i].astype(f32)
    sig = jax.nn.sigmoid(pre)
    pg[mine, :] = (hidden_grad * sig * (1.0 + pre * (1.0 - sig))).astype(bf16)
    pg_x = send(pg.at[mine, :], pg.at[mine, :], (me_b, x_n))
    pg_core = [send(pg.at[mine, :], pg.at[mine, :], (me_b, core_n))]
    hid[mine, :] = (pre * sig).astype(bf16)
    hid_x = send(hid.at[mine, :], hid.at[mine, :], (me_b, x_n))
    hid_core = [send(hid.at[mine, :], hid.at[mine, :], (me_b, core_n))]
    theirs = group_rows(x_n)
    pg_x.wait_recv()
    pg_core.append(send(pg.at[theirs, :], pg.at[theirs, :], (me_b, core_n)))
    hid_x.wait_recv()
    hid_core.append(send(hid.at[theirs, :], hid.at[theirs, :], (me_b, core_n)))
    for copy in pg_core:
        copy.wait_recv()

    contract_rows = (((0,), (0,)), ((), ()))
    tracks = (pl.ds(0, 2), pl.ds(2, 1))

    def piece_of(track, b):
        return (tracks[track], pl.ds(pl.multiple_of(b * piece, piece), piece), slice(None))

    def fill(k, left, right):
        value = lax.dot_general(left, right, contract_rows, preferred_element_type=f32)
        grad32[k] = value
        grad[k] = value.astype(bf16)

    def to_other_y(track):
        return [
            send(
                grad.at[piece_of(track, z_at(dz) * Y_SIZE + other_y)],
                from_y.at[dz, tracks[track]],
                y_dev,
            )
            for dz in z_order + [0]
        ]

    fill(0, agg[...], pg[...])
    fill(1, xf[me_b], pg[...])
    halves = [to_other_y(0)]
    for copy in hid_core:
        copy.wait_recv()
    fill(2, cot[:, slice_cols(me_n)], hid[...])
    halves.append(to_other_y(1))

    sums, arriving_z = [], []
    for track in range(2):
        along = tracks[track]
        arriving_z.append([])
        for dz, copy in zip(z_order + [0], halves[track]):
            copy.wait_recv()
            both = grad32[piece_of(track, z_at(dz) * Y_SIZE + y)] + from_y[dz, along].astype(f32)
            if dz:
                to_z[dz, along] = both.astype(bf16)
                arriving_z[track].append(
                    (dz, send(to_z.at[dz, along], from_z.at[dz, along], z_dev(dz)))
                )
        sums.append(both)
    lo[...] = jnp.dot(hid[...], ow[:, slice_cols(me_n)], preferred_element_type=f32)
    lo_copy = pltpu.make_async_copy(lo, lo_out, local_sem.at[6])
    lo_copy.start()
    last, done = [], []
    for track in range(2):
        both = sums[track]
        for dz, copy in arriving_z[track]:
            copy.wait_recv()
            both = both + from_z[dz, tracks[track]].astype(f32)
        own = piece_of(track, me_b)
        gall[own] = both.astype(bf16)
        done.append({dz: send(gall.at[own], gall.at[own], z_dev(dz)) for dz in z_order})
        last.append(send(gall.at[own], gall.at[own], y_dev))
    for track in range(2):
        for dz in z_order[1:] + z_order[:1]:
            done[track][dz].wait_recv()
            at = piece_of(track, z_source(dz))
            last.append(send(gall.at[at], gall.at[at], y_dev))
    for copy in last:
        copy.wait_recv()
    out_copy = pltpu.make_async_copy(gall, grads_out, local_sem.at[7])
    out_copy.start()
    for copy in pending:
        copy.wait_send()
    lo_copy.wait()
    out_copy.wait()


def per_device_fused(
    wide, narrow,
    features, tile_blocks, tile_rows, tile_cols, tile_count,
    neighbor_weight, root_weight, output_weight, cotangent,
):
    node_rows, width = features.shape
    hidden_width = output_weight.shape[0]
    group = node_rows // narrow
    side = tile_blocks.shape[-1]
    z_size = wide // Y_SIZE
    piece = width // wide
    bf16, f32 = jnp.bfloat16, jnp.float32
    copies = 64
    hbm = pl.BlockSpec(memory_space=pltpu.HBM)
    smem = pl.BlockSpec(memory_space=pltpu.SMEM)
    grads, product = pl.pallas_call(
        functools.partial(fused_kernel, wide, narrow),
        out_shape=(
            jax.ShapeDtypeStruct((3, width, hidden_width), bf16),
            jax.ShapeDtypeStruct((node_rows, width), f32),
        ),
        in_specs=[hbm, hbm, smem, smem, smem, hbm, hbm, hbm, hbm],
        out_specs=(hbm, hbm),
        scratch_shapes=[
            pltpu.VMEM((wide, node_rows, width), bf16),
            pltpu.VMEM(tile_blocks.shape[2:], bf16),
            pltpu.VMEM((hidden_width, hidden_width), bf16),
            pltpu.VMEM((node_rows, hidden_width), bf16),
            pltpu.VMEM((width, hidden_width), bf16),
            pltpu.VMEM((width, hidden_width), bf16),
            pltpu.VMEM((narrow, node_rows // side, side, wide * group), bf16),
            pltpu.VMEM((node_rows, hidden_width), f32),
            pltpu.VMEM((narrow - 1, group, hidden_width), bf16),
            pltpu.VMEM((narrow - 1, group, hidden_width), bf16),
            pltpu.VMEM((node_rows, width), bf16),
            pltpu.VMEM((node_rows, hidden_width), bf16),
            pltpu.VMEM((node_rows, hidden_width), bf16),
            pltpu.VMEM((3, width, hidden_width), f32),
            pltpu.VMEM((3, width, hidden_width), bf16),
            pltpu.VMEM((z_size, 3, piece, hidden_width), bf16),
            pltpu.VMEM((z_size, 3, piece, hidden_width), bf16),
            pltpu.VMEM((z_size, 3, piece, hidden_width), bf16),
            pltpu.VMEM((3, width, hidden_width), bf16),
            pltpu.VMEM((node_rows, width), f32),
            pltpu.SemaphoreType.DMA((8,)),
            pltpu.SemaphoreType.DMA((copies,)),
            pltpu.SemaphoreType.DMA((copies,)),
        ],
        compiler_params=pltpu.CompilerParams(
            collective_id=0, has_side_effects=True, vmem_limit_bytes=63 * 1024 * 1024
        ),
    )(
        features, tile_blocks, tile_rows, tile_cols, tile_count,
        neighbor_weight, root_weight, output_weight, cotangent,
    )
    layer_output = (features.astype(f32) + product).astype(bf16)
    return (
        layer_output,
        grads[0].astype(f32),
        grads[1].astype(f32),
        grads[2].T.astype(f32),
    )


def solution(mesh):
    wide, narrow = mesh.shape["wide"], mesh.shape["narrow"]
    if wide == 8 and narrow == 4:
        per_device = functools.partial(per_device_fused, wide, narrow)
    else:
        per_device = per_device_large
    return jax.shard_map(
        per_device,
        mesh=mesh,
        in_specs=(
            P("wide", "narrow"),
            P("wide", "narrow", None, None, None),
            P("wide", "narrow", None),
            P("wide", "narrow", None),
            P("wide", "narrow"),
            P("narrow", None),
            P("narrow", None),
            P(),
            P("wide", None),
        ),
        out_specs=(P("wide", "narrow"), P("narrow", None), P("narrow", None), P(None, "narrow")),
        check_vma=False,
    )
```

```python
import functools
import math

import jax
import jax.numpy as jnp
from jax import lax
from jax.experimental import pallas as pl
from jax.experimental.pallas import tpu as pltpu
from jax.sharding import PartitionSpec as P


def tile_sum(block_tiles, row_ids, col_ids, live_count, column_tiles, tile_rows_count):
    capacity = block_tiles.shape[0]
    block_size = math.gcd(capacity, 24)
    tile_side = block_tiles.shape[-1]
    feature_width = column_tiles.shape[-1]
    row_range = jnp.arange(tile_rows_count, dtype=jnp.int32)
    slot_range = jnp.arange(block_size, dtype=jnp.int32)

    def one_turn(turn_index, running):
        first_slot = turn_index * block_size
        some_tiles = lax.dynamic_slice_in_dim(block_tiles, first_slot, block_size, 0)
        some_rows = lax.dynamic_slice_in_dim(row_ids, first_slot, block_size, 0)
        some_cols = lax.dynamic_slice_in_dim(col_ids, first_slot, block_size, 0)
        picked = column_tiles[some_cols]
        product = jnp.einsum("tij,tjh->tih", some_tiles, picked, preferred_element_type=jnp.float32)
        alive = (first_slot + slot_range < live_count).astype(jnp.float32)
        placing = alive[:, None] * (some_rows[:, None] == row_range[None, :]).astype(jnp.float32)
        return running + jnp.einsum("tr,tih->rih", placing, product)

    block_turns = (live_count + block_size - 1) // block_size
    start_value = jnp.zeros((tile_rows_count, tile_side, feature_width), jnp.float32)
    summed = lax.fori_loop(0, block_turns, one_turn, start_value)
    return summed.reshape(tile_rows_count * tile_side, feature_width)


def per_device_large(
    features,
    tile_blocks,
    tile_rows,
    tile_cols,
    tile_count,
    neighbor_weight,
    root_weight,
    output_weight,
    cotangent,
):
    node_rows = features.shape[0]
    slice_width = features.shape[1]
    wide_count = lax.axis_size("wide")
    narrow_count = lax.axis_size("narrow")
    tile_side = tile_blocks.shape[-1]
    tile_rows_count = node_rows // tile_side
    group_rows = node_rows // narrow_count
    all_tiles, all_rows, all_cols, all_counts = (
        lax.all_gather(tile_blocks, "narrow", axis=1, tiled=True),
        lax.all_gather(tile_rows, "narrow", axis=1, tiled=True),
        lax.all_gather(tile_cols, "narrow", axis=1, tiled=True),
        lax.all_gather(tile_count, "narrow", axis=1, tiled=True),
    )
    columns = lax.all_gather(features, "wide", axis=0, tiled=True)
    groups = columns.reshape(wide_count, narrow_count, group_rows, slice_width).transpose(
        1, 0, 2, 3
    )
    groups = groups.reshape(narrow_count, -1, tile_side, slice_width)
    running = jnp.zeros((node_rows, slice_width), jnp.float32)
    for source in range(narrow_count):
        running = running + tile_sum(
            all_tiles[0, source],
            all_rows[0, source],
            all_cols[0, source],
            all_counts[0, source],
            groups[source],
            tile_rows_count,
        )
    agg = running.astype(jnp.bfloat16)
    partial_pre = jnp.dot(agg, neighbor_weight, preferred_element_type=jnp.float32) + jnp.dot(
        features, root_weight, preferred_element_type=jnp.float32
    )
    pre = lax.psum(partial_pre, "narrow")
    hidden = jax.nn.silu(pre).astype(jnp.bfloat16)
    narrow_index = lax.axis_index("narrow")
    out_columns = lax.dynamic_slice_in_dim(
        output_weight, narrow_index * slice_width, slice_width, 1
    )
    layer_output = (
        features.astype(jnp.float32)
        + jnp.dot(hidden, out_columns, preferred_element_type=jnp.float32)
    ).astype(jnp.bfloat16)
    hidden_grad = jnp.dot(cotangent, output_weight.T, preferred_element_type=jnp.float32)
    sigmoid_pre = jax.nn.sigmoid(pre)
    pre_grad = (hidden_grad * sigmoid_pre * (1.0 + pre * (1.0 - sigmoid_pre))).astype(jnp.bfloat16)
    cot_columns = lax.dynamic_slice_in_dim(cotangent, narrow_index * slice_width, slice_width, 1)
    neighbor_part = jnp.dot(agg.T, pre_grad, preferred_element_type=jnp.float32)
    root_part = jnp.dot(features.T, pre_grad, preferred_element_type=jnp.float32)
    output_part = jnp.dot(hidden.T, cot_columns, preferred_element_type=jnp.float32)
    neighbor_grad, root_grad, output_grad = lax.psum(
        (neighbor_part, root_part, output_part), "wide"
    )
    return (layer_output, neighbor_grad, root_grad, output_grad)


Y_SIZE = 2
CORES = 2
MESH = pl.DeviceIdType.MESH


def fused_kernel(
    wide, narrow,
    x_hbm, t_hbm, rows_ref, cols_ref, count_hbm, wn_hbm, wr_hbm, ow_hbm, cot_hbm,
    grads_out, lo_out,
    xf, tiles, ow, cot, wn, wr, count_ref, dense, part, hidden_grad, sent, came, pre_all, agg,
    pg, hid, grad32, grad, from_y, to_z, from_z, gall, lo,
    local_sem, send_sem, recv_sem,
):
    z_size = wide // Y_SIZE
    me_b = lax.axis_index("wide")
    me_n = lax.axis_index("narrow")
    z, y = me_b // Y_SIZE, me_b % Y_SIZE
    other_y = 1 - y
    core_n = me_n // CORES * CORES + (1 - me_n % CORES)
    x_n = (me_n + CORES) % narrow
    xc_n = (core_n + CORES) % narrow
    node_rows, width = x_hbm.shape
    hidden_width = ow_hbm.shape[0]
    group = node_rows // narrow
    side = t_hbm.shape[-1]
    slots = t_hbm.shape[2]
    piece = width // wide
    tile_rows_count = node_rows // side
    across = dense.shape[-1] // side
    f32, bf16 = jnp.float32, jnp.bfloat16
    y_dev = (z * Y_SIZE + other_y, me_n)

    def group_rows(n):
        return pl.ds(pl.multiple_of(n * group, group), group)

    def slice_cols(n):
        return pl.ds(pl.multiple_of(n * width, width), width)

    def z_at(dz):
        return lax.rem(z + dz, z_size)

    def z_dev(dz):
        return (z_at(dz) * Y_SIZE + y, me_n)

    def z_source(dz):
        return lax.rem(z + z_size - dz, z_size) * Y_SIZE + y

    used = [0]
    pending = []

    def send(src, dst, device):
        k = used[0]
        used[0] += 1
        copy = pltpu.make_async_remote_copy(
            src_ref=src, dst_ref=dst, send_sem=send_sem.at[k], recv_sem=recv_sem.at[k],
            device_id=device, device_id_type=MESH,
        )
        copy.start()
        pending.append(copy)
        return copy

    barrier = pltpu.get_barrier_semaphore()
    partners = [(me_b, n) for n in (core_n, x_n, xc_n)]
    partners += [z_dev(dz) for dz in range(1, z_size)] + [y_dev]
    for device in partners:
        pl.semaphore_signal(barrier, inc=1, device_id=device, device_id_type=MESH)

    local = [
        pltpu.make_async_copy(src, dst, local_sem.at[k])
        for k, (src, dst) in enumerate(
            (
                (count_hbm, count_ref),
                (t_hbm.at[0, 0], tiles),
                (x_hbm, xf.at[me_b]),
                (wr_hbm, wr),
                (wn_hbm, wn),
                (cot_hbm, cot),
                (ow_hbm, ow),
            )
        )
    ]
    for copy in local:
        copy.start()
    count_copy, tile_copy, x_copy, wr_copy, wn_copy, cot_copy, ow_copy = local

    count_copy.wait()
    live = count_ref[0, 0]
    chunk = 32
    positions = tile_rows_count * across
    steps = side // chunk

    def densify(step, _):
        at = pl.ds(pl.multiple_of(step * chunk, chunk), chunk)

        def add_slot(s, sums):
            tile = tiles[s, at, :].astype(f32)
            place = rows_ref[0, 0, s] * across + cols_ref[0, 0, s]
            place = jnp.where(s < live, place, -1)
            return tuple(
                sums[p] + tile * jnp.where(place == p, 1.0, 0.0).astype(f32)
                for p in range(positions)
            )

        sums = lax.fori_loop(
            0, slots, add_slot,
            tuple(jnp.zeros((chunk, side), f32) for _ in range(positions)),
            unroll=4,
        )
        for p in range(positions):
            dense[me_n, p // across, at, pl.ds(p % across * side, side)] = sums[p].astype(bf16)
        return 0

    def half(n, h):
        return dense.at[n, :, pl.ds(h * (side // 2), side // 2), :]

    tile_copy.wait()
    lax.fori_loop(0, steps // 2, densify, 0)
    pl.semaphore_wait(barrier, len(partners))

    z_order = sorted(range(1, z_size), key=lambda dz: abs(dz - z_size / 2))
    x_halves = [pl.ds(h * (node_rows // 2), node_rows // 2) for h in range(2)]
    blocks = {
        (dz, h): send(x_hbm.at[x_halves[h]], xf.at[me_b, x_halves[h]], z_dev(dz))
        for h in range(2)
        for dz in z_order
    }
    y_blocks = [send(x_hbm, xf.at[me_b], y_dev)]
    dense_x = [send(half(me_n, 0), half(me_n, 0), (me_b, x_n))]
    dense_core = [send(half(me_n, 0), half(me_n, 0), (me_b, core_n))]
    lax.fori_loop(steps // 2, steps, densify, 0)
    dense_x.append(send(half(me_n, 1), half(me_n, 1), (me_b, x_n)))
    dense_core.append(send(half(me_n, 1), half(me_n, 1), (me_b, core_n)))
    dense_fwd = []

    def pass_block(dz, h):
        blocks[dz, h].wait_recv()
        part_of = xf.at[z_source(dz), x_halves[h]]
        y_blocks.append(send(part_of, part_of, y_dev))

    def pass_half(h):
        dense_x[h].wait_recv()
        dense_fwd.append(send(half(x_n, h), half(x_n, h), (me_b, core_n)))

    for dz in z_order[1:] + z_order[:1]:
        pass_block(dz, 0)
    pass_half(0)
    for dz in z_order[1:] + z_order[:1]:
        pass_block(dz, 1)
    cot_copy.wait()
    ow_copy.wait()
    hidden_grad[...] = lax.dot_general(
        cot[...], ow[...], (((1,), (1,)), ((), ())), preferred_element_type=f32
    )
    pass_half(1)
    x_copy.wait()
    wr_copy.wait()
    wn_copy.wait()
    part[...] = jnp.dot(xf[me_b], wr[...], preferred_element_type=f32)

    for copy in y_blocks:
        copy.wait_recv()

    def product(n):
        column_tiles = xf[:, group_rows(n), :].reshape(wide * group, width)
        return jnp.dot(
            dense[n].reshape(node_rows, wide * group), column_tiles, preferred_element_type=f32
        )

    total = product(me_n)
    for copy in dense_core:
        copy.wait_recv()
    total = total + product(core_n)
    total = total + product(x_n)
    for copy in dense_fwd:
        copy.wait_recv()
    total = total + product(xc_n)
    agg[...] = total.astype(bf16)

    def pre_rows(core, q):
        return pl.ds(pl.multiple_of(core * 2 * group + q * group, group), group)

    def gates(rows, pre):
        sig = jax.nn.sigmoid(pre)
        pg[rows, :] = (hidden_grad[rows, :] * sig * (1.0 + pre * (1.0 - sig))).astype(bf16)
        hid[rows, :] = (pre * sig).astype(bf16)

    def half_pre(core):
        rows = pl.ds(pl.multiple_of(core * 2 * group, group), 2 * group)
        return part[rows, :] + jnp.dot(agg[rows, :], wn[...], preferred_element_type=f32)

    my_core = me_n % CORES
    sent[0] = half_pre(1 - my_core).astype(bf16).reshape(2, group, hidden_width)
    to_core = [send(sent.at[0, q], came.at[0, q], (me_b, core_n)) for q in range(2)]
    kept = half_pre(my_core).reshape(2, group, hidden_width)
    kept = [kept[0], kept[1]]
    to_x, back = [], []
    for q in range(2):
        to_core[q].wait_recv()
        kept[q] = kept[q] + came[0, q].astype(f32)
        sent[1, q] = kept[q].astype(bf16)
        to_x.append(send(sent.at[1, q], came.at[1, q], (me_b, x_n)))
    for q in range(2):
        to_x[q].wait_recv()
        pre = kept[q] + came[1, q].astype(f32)
        rows = pre_rows(my_core, q)
        pre_all[rows, :] = pre.astype(bf16)
        back.append(send(pre_all.at[rows, :], pre_all.at[rows, :], (me_b, core_n)))
        gates(rows, pre)
    for q in range(2):
        back[q].wait_recv()
        rows = pre_rows(1 - my_core, q)
        gates(rows, pre_all[rows, :].astype(f32))

    contract_rows = (((0,), (0,)), ((), ()))
    tracks = (pl.ds(0, 2), pl.ds(2, 1))

    def piece_of(track, b):
        return (tracks[track], pl.ds(pl.multiple_of(b * piece, piece), piece), slice(None))

    def fill(k, left, right):
        value = lax.dot_general(left, right, contract_rows, preferred_element_type=f32)
        grad32[k] = value
        grad[k] = value.astype(bf16)

    def to_other_y(track):
        return [
            send(
                grad.at[piece_of(track, z_at(dz) * Y_SIZE + other_y)],
                from_y.at[dz, tracks[track]],
                y_dev,
            )
            for dz in z_order + [0]
        ]

    fill(0, agg[...], pg[...])
    fill(1, xf[me_b], pg[...])
    halves = [to_other_y(0)]
    fill(2, cot[:, slice_cols(me_n)], hid[...])
    halves.append(to_other_y(1))

    sums, arriving_z = [], []
    for track in range(2):
        along = tracks[track]
        arriving_z.append([])
        for dz, copy in zip(z_order + [0], halves[track]):
            copy.wait_recv()
            both = grad32[piece_of(track, z_at(dz) * Y_SIZE + y)] + from_y[dz, along].astype(f32)
            if dz:
                to_z[dz, along] = both.astype(bf16)
                arriving_z[track].append(
                    (dz, send(to_z.at[dz, along], from_z.at[dz, along], z_dev(dz)))
                )
        sums.append(both)
    lo[...] = jnp.dot(hid[...], ow[:, slice_cols(me_n)], preferred_element_type=f32)
    lo_copy = pltpu.make_async_copy(lo, lo_out, local_sem.at[7])
    lo_copy.start()
    last, done = [], []
    for track in range(2):
        both = sums[track]
        for dz, copy in arriving_z[track]:
            copy.wait_recv()
            both = both + from_z[dz, tracks[track]].astype(f32)
        own = piece_of(track, me_b)
        gall[own] = both.astype(bf16)
        done.append({dz: send(gall.at[own], gall.at[own], z_dev(dz)) for dz in z_order})
        last.append(send(gall.at[own], gall.at[own], y_dev))
    for track in range(2):
        for dz in z_order[1:] + z_order[:1]:
            done[track][dz].wait_recv()
            at = piece_of(track, z_source(dz))
            last.append(send(gall.at[at], gall.at[at], y_dev))
    for copy in last:
        copy.wait_recv()
    out_copy = pltpu.make_async_copy(gall, grads_out, local_sem.at[8])
    out_copy.start()
    for copy in pending:
        copy.wait_send()
    lo_copy.wait()
    out_copy.wait()


def finish_kernel(x_ref, product_ref, grads_ref, out_ref, neighbor_ref, root_ref, output_ref):
    f32 = jnp.float32
    out_ref[...] = (x_ref[...].astype(f32) + product_ref[...]).astype(out_ref.dtype)
    neighbor_ref[...] = grads_ref[0].astype(f32)
    root_ref[...] = grads_ref[1].astype(f32)
    output_ref[...] = grads_ref[2].astype(f32).T


def per_device_fused(
    wide, narrow,
    features, tile_blocks, tile_rows, tile_cols, tile_count,
    neighbor_weight, root_weight, output_weight, cotangent,
):
    node_rows, width = features.shape
    hidden_width = output_weight.shape[0]
    group = node_rows // narrow
    side = tile_blocks.shape[-1]
    z_size = wide // Y_SIZE
    piece = width // wide
    bf16, f32 = jnp.bfloat16, jnp.float32
    copies = 64
    hbm = pl.BlockSpec(memory_space=pltpu.HBM)
    smem = pl.BlockSpec(memory_space=pltpu.SMEM)
    grads, product = pl.pallas_call(
        functools.partial(fused_kernel, wide, narrow),
        out_shape=(
            jax.ShapeDtypeStruct((3, width, hidden_width), bf16),
            jax.ShapeDtypeStruct((node_rows, width), f32),
        ),
        in_specs=[hbm, hbm, smem, smem, hbm, hbm, hbm, hbm, hbm],
        out_specs=(hbm, hbm),
        scratch_shapes=[
            pltpu.VMEM((wide, node_rows, width), bf16),
            pltpu.VMEM(tile_blocks.shape[2:], bf16),
            pltpu.VMEM((hidden_width, hidden_width), bf16),
            pltpu.VMEM((node_rows, hidden_width), bf16),
            pltpu.VMEM((width, hidden_width), bf16),
            pltpu.VMEM((width, hidden_width), bf16),
            pltpu.SMEM(tile_count.shape, jnp.int32),
            pltpu.VMEM((narrow, node_rows // side, side, wide * group), bf16),
            pltpu.VMEM((node_rows, hidden_width), f32),
            pltpu.VMEM((node_rows, hidden_width), f32),
            pltpu.VMEM((2, 2, group, hidden_width), bf16),
            pltpu.VMEM((2, 2, group, hidden_width), bf16),
            pltpu.VMEM((node_rows, hidden_width), bf16),
            pltpu.VMEM((node_rows, width), bf16),
            pltpu.VMEM((node_rows, hidden_width), bf16),
            pltpu.VMEM((node_rows, hidden_width), bf16),
            pltpu.VMEM((3, width, hidden_width), f32),
            pltpu.VMEM((3, width, hidden_width), bf16),
            pltpu.VMEM((z_size, 3, piece, hidden_width), bf16),
            pltpu.VMEM((z_size, 3, piece, hidden_width), bf16),
            pltpu.VMEM((z_size, 3, piece, hidden_width), bf16),
            pltpu.VMEM((3, width, hidden_width), bf16),
            pltpu.VMEM((node_rows, width), f32),
            pltpu.SemaphoreType.DMA((9,)),
            pltpu.SemaphoreType.DMA((copies,)),
            pltpu.SemaphoreType.DMA((copies,)),
        ],
        compiler_params=pltpu.CompilerParams(
            collective_id=0, has_side_effects=True, vmem_limit_bytes=63 * 1024 * 1024
        ),
    )(
        features, tile_blocks, tile_rows, tile_cols, tile_count,
        neighbor_weight, root_weight, output_weight, cotangent,
    )
    vmem = pl.BlockSpec(memory_space=pltpu.VMEM)
    return pl.pallas_call(
        finish_kernel,
        out_shape=(
            jax.ShapeDtypeStruct((node_rows, width), bf16),
            jax.ShapeDtypeStruct((width, hidden_width), f32),
            jax.ShapeDtypeStruct((width, hidden_width), f32),
            jax.ShapeDtypeStruct((hidden_width, width), f32),
        ),
        in_specs=[vmem] * 3,
        out_specs=(vmem,) * 4,
        compiler_params=pltpu.CompilerParams(vmem_limit_bytes=63 * 1024 * 1024),
    )(features, product, grads)


def solution(mesh):
    wide, narrow = mesh.shape["wide"], mesh.shape["narrow"]
    if wide == 8 and narrow == 4:
        per_device = functools.partial(per_device_fused, wide, narrow)
    else:
        per_device = per_device_large
    return jax.shard_map(
        per_device,
        mesh=mesh,
        in_specs=(
            P("wide", "narrow"),
            P("wide", "narrow", None, None, None),
            P("wide", "narrow", None),
            P("wide", "narrow", None),
            P("wide", "narrow"),
            P("narrow", None),
            P("narrow", None),
            P(),
            P("wide", None),
        ),
        out_specs=(P("wide", "narrow"), P("narrow", None), P("narrow", None), P(None, "narrow")),
        check_vma=False,
    )
```

```python
import functools
import math

import jax
import jax.numpy as jnp
from jax import lax
from jax.experimental import pallas as pl
from jax.experimental.pallas import tpu as pltpu
from jax.sharding import PartitionSpec as P


def tile_sum(block_tiles, row_ids, col_ids, live_count, column_tiles, tile_rows_count):
    capacity = block_tiles.shape[0]
    block_size = math.gcd(capacity, 24)
    tile_side = block_tiles.shape[-1]
    feature_width = column_tiles.shape[-1]
    row_range = jnp.arange(tile_rows_count, dtype=jnp.int32)
    slot_range = jnp.arange(block_size, dtype=jnp.int32)

    def one_turn(turn_index, running):
        first_slot = turn_index * block_size
        some_tiles = lax.dynamic_slice_in_dim(block_tiles, first_slot, block_size, 0)
        some_rows = lax.dynamic_slice_in_dim(row_ids, first_slot, block_size, 0)
        some_cols = lax.dynamic_slice_in_dim(col_ids, first_slot, block_size, 0)
        picked = column_tiles[some_cols]
        product = jnp.einsum("tij,tjh->tih", some_tiles, picked, preferred_element_type=jnp.float32)
        alive = (first_slot + slot_range < live_count).astype(jnp.float32)
        placing = alive[:, None] * (some_rows[:, None] == row_range[None, :]).astype(jnp.float32)
        return running + jnp.einsum("tr,tih->rih", placing, product)

    block_turns = (live_count + block_size - 1) // block_size
    start_value = jnp.zeros((tile_rows_count, tile_side, feature_width), jnp.float32)
    summed = lax.fori_loop(0, block_turns, one_turn, start_value)
    return summed.reshape(tile_rows_count * tile_side, feature_width)


def per_device_large(
    features,
    tile_blocks,
    tile_rows,
    tile_cols,
    tile_count,
    neighbor_weight,
    root_weight,
    output_weight,
    cotangent,
):
    node_rows = features.shape[0]
    slice_width = features.shape[1]
    wide_count = lax.axis_size("wide")
    narrow_count = lax.axis_size("narrow")
    tile_side = tile_blocks.shape[-1]
    tile_rows_count = node_rows // tile_side
    group_rows = node_rows // narrow_count
    all_tiles, all_rows, all_cols, all_counts = (
        lax.all_gather(tile_blocks, "narrow", axis=1, tiled=True),
        lax.all_gather(tile_rows, "narrow", axis=1, tiled=True),
        lax.all_gather(tile_cols, "narrow", axis=1, tiled=True),
        lax.all_gather(tile_count, "narrow", axis=1, tiled=True),
    )
    columns = lax.all_gather(features, "wide", axis=0, tiled=True)
    groups = columns.reshape(wide_count, narrow_count, group_rows, slice_width).transpose(
        1, 0, 2, 3
    )
    groups = groups.reshape(narrow_count, -1, tile_side, slice_width)
    running = jnp.zeros((node_rows, slice_width), jnp.float32)
    for source in range(narrow_count):
        running = running + tile_sum(
            all_tiles[0, source],
            all_rows[0, source],
            all_cols[0, source],
            all_counts[0, source],
            groups[source],
            tile_rows_count,
        )
    agg = running.astype(jnp.bfloat16)
    partial_pre = jnp.dot(agg, neighbor_weight, preferred_element_type=jnp.float32) + jnp.dot(
        features, root_weight, preferred_element_type=jnp.float32
    )
    pre = lax.psum(partial_pre, "narrow")
    hidden = jax.nn.silu(pre).astype(jnp.bfloat16)
    narrow_index = lax.axis_index("narrow")
    out_columns = lax.dynamic_slice_in_dim(
        output_weight, narrow_index * slice_width, slice_width, 1
    )
    layer_output = (
        features.astype(jnp.float32)
        + jnp.dot(hidden, out_columns, preferred_element_type=jnp.float32)
    ).astype(jnp.bfloat16)
    hidden_grad = jnp.dot(cotangent, output_weight.T, preferred_element_type=jnp.float32)
    sigmoid_pre = jax.nn.sigmoid(pre)
    pre_grad = (hidden_grad * sigmoid_pre * (1.0 + pre * (1.0 - sigmoid_pre))).astype(jnp.bfloat16)
    cot_columns = lax.dynamic_slice_in_dim(cotangent, narrow_index * slice_width, slice_width, 1)
    neighbor_part = jnp.dot(agg.T, pre_grad, preferred_element_type=jnp.float32)
    root_part = jnp.dot(features.T, pre_grad, preferred_element_type=jnp.float32)
    output_part = jnp.dot(hidden.T, cot_columns, preferred_element_type=jnp.float32)
    neighbor_grad, root_grad, output_grad = lax.psum(
        (neighbor_part, root_part, output_part), "wide"
    )
    return (layer_output, neighbor_grad, root_grad, output_grad)


Y_SIZE = 2
CORES = 2
MESH = pl.DeviceIdType.MESH


def fused_kernel(
    wide, narrow,
    x_hbm, t_hbm, rows_ref, cols_ref, count_hbm, wn_hbm, wr_hbm, ow_hbm, cot_hbm,
    grads_out, lo_out,
    xf, tiles, ow, cot, wn, wr, count_ref, dense, part, hidden_grad, sent, came, pre_all, agg,
    pg, hid, grad32, grad, from_y, to_z, from_z, gall, lo,
    local_sem, send_sem, recv_sem,
):
    z_size = wide // Y_SIZE
    me_b = lax.axis_index("wide")
    me_n = lax.axis_index("narrow")
    z, y = me_b // Y_SIZE, me_b % Y_SIZE
    other_y = 1 - y
    core_n = me_n // CORES * CORES + (1 - me_n % CORES)
    x_n = (me_n + CORES) % narrow
    xc_n = (core_n + CORES) % narrow
    node_rows, width = x_hbm.shape
    hidden_width = ow_hbm.shape[0]
    group = node_rows // narrow
    side = t_hbm.shape[-1]
    slots = t_hbm.shape[2]
    piece = width // wide
    tile_rows_count = node_rows // side
    across = dense.shape[-1] // side
    f32, bf16 = jnp.float32, jnp.bfloat16
    y_dev = (z * Y_SIZE + other_y, me_n)

    def group_rows(n):
        return pl.ds(pl.multiple_of(n * group, group), group)

    def slice_cols(n):
        return pl.ds(pl.multiple_of(n * width, width), width)

    def z_at(dz):
        return lax.rem(z + dz, z_size)

    def z_dev(dz):
        return (z_at(dz) * Y_SIZE + y, me_n)

    def z_source(dz):
        return lax.rem(z + z_size - dz, z_size) * Y_SIZE + y

    used = [0]
    pending = []

    def send(src, dst, device):
        k = used[0]
        used[0] += 1
        copy = pltpu.make_async_remote_copy(
            src_ref=src, dst_ref=dst, send_sem=send_sem.at[k], recv_sem=recv_sem.at[k],
            device_id=device, device_id_type=MESH,
        )
        copy.start()
        pending.append(copy)
        return copy

    barrier = pltpu.get_barrier_semaphore()
    partners = [(me_b, n) for n in (core_n, x_n, xc_n)]
    partners += [z_dev(dz) for dz in range(1, z_size)] + [y_dev]
    for device in partners:
        pl.semaphore_signal(barrier, inc=1, device_id=device, device_id_type=MESH)

    local = [
        pltpu.make_async_copy(src, dst, local_sem.at[k])
        for k, (src, dst) in enumerate(
            (
                (count_hbm, count_ref),
                (t_hbm.at[0, 0], tiles),
                (x_hbm, xf.at[me_b]),
                (wr_hbm, wr),
                (wn_hbm, wn),
                (cot_hbm, cot),
                (ow_hbm, ow),
            )
        )
    ]
    for copy in local:
        copy.start()
    count_copy, tile_copy, x_copy, wr_copy, wn_copy, cot_copy, ow_copy = local

    count_copy.wait()
    live = count_ref[0, 0]
    chunk = 32
    positions = tile_rows_count * across
    steps = side // chunk

    def densify(step):
        at = pl.ds(step * chunk, chunk)

        def add_slot(s, sums):
            tile = tiles[s, at, :].astype(f32)
            place = rows_ref[0, 0, s] * across + cols_ref[0, 0, s]
            place = jnp.where(s < live, place, -1)
            return tuple(
                sums[p] + tile * jnp.where(place == p, 1.0, 0.0).astype(f32)
                for p in range(positions)
            )

        sums = lax.fori_loop(
            0, slots, add_slot,
            tuple(jnp.zeros((chunk, side), f32) for _ in range(positions)),
            unroll=4,
        )
        for p in range(positions):
            dense[me_n, p // across, at, pl.ds(p % across * side, side)] = sums[p].astype(bf16)

    def slab(n, step):
        return dense.at[n, :, pl.ds(step * chunk, chunk), :]

    pl.semaphore_wait(barrier, len(partners))
    z_order = sorted(range(1, z_size), key=lambda dz: abs(dz - z_size / 2))
    x_halves = [pl.ds(h * (node_rows // 2), node_rows // 2) for h in range(2)]
    blocks = {
        (dz, h): send(x_hbm.at[x_halves[h]], xf.at[me_b, x_halves[h]], z_dev(dz))
        for h in range(2)
        for dz in z_order
    }
    y_blocks = [send(x_hbm, xf.at[me_b], y_dev)]
    tile_copy.wait()
    dense_x, dense_core, dense_fwd = [], [], []
    for step in range(steps):
        densify(step)
        dense_x.append(send(slab(me_n, step), slab(me_n, step), (me_b, x_n)))
        dense_core.append(send(slab(me_n, step), slab(me_n, step), (me_b, core_n)))

    def pass_block(dz, h):
        blocks[dz, h].wait_recv()
        part_of = xf.at[z_source(dz), x_halves[h]]
        y_blocks.append(send(part_of, part_of, y_dev))

    def pass_slab(step):
        dense_x[step].wait_recv()
        dense_fwd.append(send(slab(x_n, step), slab(x_n, step), (me_b, core_n)))

    for dz in z_order[1:] + z_order[:1]:
        pass_block(dz, 0)
    for step in range(steps // 2):
        pass_slab(step)
    cot_copy.wait()
    ow_copy.wait()
    hidden_grad[...] = lax.dot_general(
        cot[...], ow[...], (((1,), (1,)), ((), ())), preferred_element_type=f32
    )
    for dz in z_order[1:] + z_order[:1]:
        pass_block(dz, 1)
    for step in range(steps // 2, steps):
        pass_slab(step)
    x_copy.wait()
    wr_copy.wait()
    wn_copy.wait()
    part[...] = jnp.dot(xf[me_b], wr[...], preferred_element_type=f32)

    for copy in y_blocks:
        copy.wait_recv()

    def product(n):
        column_tiles = xf[:, group_rows(n), :].reshape(wide * group, width)
        return jnp.dot(
            dense[n].reshape(node_rows, wide * group), column_tiles, preferred_element_type=f32
        )

    total = product(me_n)
    for copy in dense_core:
        copy.wait_recv()
    total = total + product(core_n)
    total = total + product(x_n)
    for copy in dense_fwd:
        copy.wait_recv()
    total = total + product(xc_n)
    agg[...] = total.astype(bf16)

    def pre_rows(core, q):
        return pl.ds(pl.multiple_of(core * 2 * group + q * group, group), group)

    def gates(rows, pre):
        sig = jax.nn.sigmoid(pre)
        pg[rows, :] = (hidden_grad[rows, :] * sig * (1.0 + pre * (1.0 - sig))).astype(bf16)
        hid[rows, :] = (pre * sig).astype(bf16)

    def half_pre(core):
        rows = pl.ds(pl.multiple_of(core * 2 * group, group), 2 * group)
        return part[rows, :] + jnp.dot(agg[rows, :], wn[...], preferred_element_type=f32)

    my_core = me_n % CORES
    sent[0] = half_pre(1 - my_core).astype(bf16).reshape(2, group, hidden_width)
    to_core = [send(sent.at[0, q], came.at[0, q], (me_b, core_n)) for q in range(2)]
    kept = half_pre(my_core).reshape(2, group, hidden_width)
    kept = [kept[0], kept[1]]
    to_x, back = [], []
    for q in range(2):
        to_core[q].wait_recv()
        kept[q] = kept[q] + came[0, q].astype(f32)
        sent[1, q] = kept[q].astype(bf16)
        to_x.append(send(sent.at[1, q], came.at[1, q], (me_b, x_n)))
    for q in range(2):
        to_x[q].wait_recv()
        pre = kept[q] + came[1, q].astype(f32)
        rows = pre_rows(my_core, q)
        pre_all[rows, :] = pre.astype(bf16)
        back.append(send(pre_all.at[rows, :], pre_all.at[rows, :], (me_b, core_n)))
        gates(rows, pre)
    for q in range(2):
        back[q].wait_recv()
        rows = pre_rows(1 - my_core, q)
        gates(rows, pre_all[rows, :].astype(f32))

    contract_rows = (((0,), (0,)), ((), ()))
    tracks = (pl.ds(0, 2), pl.ds(2, 1))

    def piece_of(track, b):
        return (tracks[track], pl.ds(pl.multiple_of(b * piece, piece), piece), slice(None))

    def fill(k, left, right):
        value = lax.dot_general(left, right, contract_rows, preferred_element_type=f32)
        grad32[k] = value
        grad[k] = value.astype(bf16)

    def to_other_y(track):
        return [
            send(
                grad.at[piece_of(track, z_at(dz) * Y_SIZE + other_y)],
                from_y.at[dz, tracks[track]],
                y_dev,
            )
            for dz in z_order + [0]
        ]

    fill(0, agg[...], pg[...])
    fill(1, xf[me_b], pg[...])
    halves = [to_other_y(0)]
    fill(2, cot[:, slice_cols(me_n)], hid[...])
    halves.append(to_other_y(1))

    sums, arriving_z = [], []
    for track in range(2):
        along = tracks[track]
        arriving_z.append([])
        for dz, copy in zip(z_order + [0], halves[track]):
            copy.wait_recv()
            both = grad32[piece_of(track, z_at(dz) * Y_SIZE + y)] + from_y[dz, along].astype(f32)
            if dz:
                to_z[dz, along] = both.astype(bf16)
                arriving_z[track].append(
                    (dz, send(to_z.at[dz, along], from_z.at[dz, along], z_dev(dz)))
                )
        sums.append(both)
    lo[...] = jnp.dot(hid[...], ow[:, slice_cols(me_n)], preferred_element_type=f32)
    lo_copy = pltpu.make_async_copy(lo, lo_out, local_sem.at[7])
    lo_copy.start()
    last, done = [], []
    for track in range(2):
        both = sums[track]
        for dz, copy in arriving_z[track]:
            copy.wait_recv()
            both = both + from_z[dz, tracks[track]].astype(f32)
        own = piece_of(track, me_b)
        gall[own] = both.astype(bf16)
        done.append({dz: send(gall.at[own], gall.at[own], z_dev(dz)) for dz in z_order})
        last.append(send(gall.at[own], gall.at[own], y_dev))
    for track in range(2):
        for dz in z_order[1:] + z_order[:1]:
            done[track][dz].wait_recv()
            at = piece_of(track, z_source(dz))
            last.append(send(gall.at[at], gall.at[at], y_dev))
    for copy in last:
        copy.wait_recv()
    out_copy = pltpu.make_async_copy(gall, grads_out, local_sem.at[8])
    out_copy.start()
    for copy in pending:
        copy.wait_send()
    lo_copy.wait()
    out_copy.wait()


def finish_kernel(x_ref, product_ref, grads_ref, out_ref, neighbor_ref, root_ref, output_ref):
    f32 = jnp.float32
    out_ref[...] = (x_ref[...].astype(f32) + product_ref[...]).astype(out_ref.dtype)
    neighbor_ref[...] = grads_ref[0].astype(f32)
    root_ref[...] = grads_ref[1].astype(f32)
    output_ref[...] = grads_ref[2].astype(f32).T


def per_device_fused(
    wide, narrow,
    features, tile_blocks, tile_rows, tile_cols, tile_count,
    neighbor_weight, root_weight, output_weight, cotangent,
):
    node_rows, width = features.shape
    hidden_width = output_weight.shape[0]
    group = node_rows // narrow
    side = tile_blocks.shape[-1]
    z_size = wide // Y_SIZE
    piece = width // wide
    bf16, f32 = jnp.bfloat16, jnp.float32
    copies = 64
    hbm = pl.BlockSpec(memory_space=pltpu.HBM)
    smem = pl.BlockSpec(memory_space=pltpu.SMEM)
    grads, product = pl.pallas_call(
        functools.partial(fused_kernel, wide, narrow),
        out_shape=(
            jax.ShapeDtypeStruct((3, width, hidden_width), bf16),
            jax.ShapeDtypeStruct((node_rows, width), f32),
        ),
        in_specs=[hbm, hbm, smem, smem, hbm, hbm, hbm, hbm, hbm],
        out_specs=(hbm, hbm),
        scratch_shapes=[
            pltpu.VMEM((wide, node_rows, width), bf16),
            pltpu.VMEM(tile_blocks.shape[2:], bf16),
            pltpu.VMEM((hidden_width, hidden_width), bf16),
            pltpu.VMEM((node_rows, hidden_width), bf16),
            pltpu.VMEM((width, hidden_width), bf16),
            pltpu.VMEM((width, hidden_width), bf16),
            pltpu.SMEM(tile_count.shape, jnp.int32),
            pltpu.VMEM((narrow, node_rows // side, side, wide * group), bf16),
            pltpu.VMEM((node_rows, hidden_width), f32),
            pltpu.VMEM((node_rows, hidden_width), f32),
            pltpu.VMEM((2, 2, group, hidden_width), bf16),
            pltpu.VMEM((2, 2, group, hidden_width), bf16),
            pltpu.VMEM((node_rows, hidden_width), bf16),
            pltpu.VMEM((node_rows, width), bf16),
            pltpu.VMEM((node_rows, hidden_width), bf16),
            pltpu.VMEM((node_rows, hidden_width), bf16),
            pltpu.VMEM((3, width, hidden_width), f32),
            pltpu.VMEM((3, width, hidden_width), bf16),
            pltpu.VMEM((z_size, 3, piece, hidden_width), bf16),
            pltpu.VMEM((z_size, 3, piece, hidden_width), bf16),
            pltpu.VMEM((z_size, 3, piece, hidden_width), bf16),
            pltpu.VMEM((3, width, hidden_width), bf16),
            pltpu.VMEM((node_rows, width), f32),
            pltpu.SemaphoreType.DMA((9,)),
            pltpu.SemaphoreType.DMA((copies,)),
            pltpu.SemaphoreType.DMA((copies,)),
        ],
        compiler_params=pltpu.CompilerParams(
            collective_id=0, has_side_effects=True, vmem_limit_bytes=63 * 1024 * 1024
        ),
    )(
        features, tile_blocks, tile_rows, tile_cols, tile_count,
        neighbor_weight, root_weight, output_weight, cotangent,
    )
    vmem = pl.BlockSpec(memory_space=pltpu.VMEM)
    return pl.pallas_call(
        finish_kernel,
        out_shape=(
            jax.ShapeDtypeStruct((node_rows, width), bf16),
            jax.ShapeDtypeStruct((width, hidden_width), f32),
            jax.ShapeDtypeStruct((width, hidden_width), f32),
            jax.ShapeDtypeStruct((hidden_width, width), f32),
        ),
        in_specs=[vmem] * 3,
        out_specs=(vmem,) * 4,
        compiler_params=pltpu.CompilerParams(vmem_limit_bytes=63 * 1024 * 1024),
    )(features, product, grads)


def solution(mesh):
    wide, narrow = mesh.shape["wide"], mesh.shape["narrow"]
    if wide == 8 and narrow == 4:
        per_device = functools.partial(per_device_fused, wide, narrow)
    else:
        per_device = per_device_large
    return jax.shard_map(
        per_device,
        mesh=mesh,
        in_specs=(
            P("wide", "narrow"),
            P("wide", "narrow", None, None, None),
            P("wide", "narrow", None),
            P("wide", "narrow", None),
            P("wide", "narrow"),
            P("narrow", None),
            P("narrow", None),
            P(),
            P("wide", None),
        ),
        out_specs=(P("wide", "narrow"), P("narrow", None), P("narrow", None), P(None, "narrow")),
        check_vma=False,
    )
```

```python
import functools
import math

import jax
import jax.numpy as jnp
from jax import lax
from jax.experimental import pallas as pl
from jax.experimental.pallas import tpu as pltpu
from jax.sharding import PartitionSpec as P


def tile_sum(block_tiles, row_ids, col_ids, live_count, column_tiles, tile_rows_count):
    capacity = block_tiles.shape[0]
    block_size = math.gcd(capacity, 24)
    tile_side = block_tiles.shape[-1]
    feature_width = column_tiles.shape[-1]
    row_range = jnp.arange(tile_rows_count, dtype=jnp.int32)
    slot_range = jnp.arange(block_size, dtype=jnp.int32)

    def one_turn(turn_index, running):
        first_slot = turn_index * block_size
        some_tiles = lax.dynamic_slice_in_dim(block_tiles, first_slot, block_size, 0)
        some_rows = lax.dynamic_slice_in_dim(row_ids, first_slot, block_size, 0)
        some_cols = lax.dynamic_slice_in_dim(col_ids, first_slot, block_size, 0)
        picked = column_tiles[some_cols]
        product = jnp.einsum("tij,tjh->tih", some_tiles, picked, preferred_element_type=jnp.float32)
        alive = (first_slot + slot_range < live_count).astype(jnp.float32)
        placing = alive[:, None] * (some_rows[:, None] == row_range[None, :]).astype(jnp.float32)
        return running + jnp.einsum("tr,tih->rih", placing, product)

    block_turns = (live_count + block_size - 1) // block_size
    start_value = jnp.zeros((tile_rows_count, tile_side, feature_width), jnp.float32)
    summed = lax.fori_loop(0, block_turns, one_turn, start_value)
    return summed.reshape(tile_rows_count * tile_side, feature_width)


def per_device_large(
    features,
    tile_blocks,
    tile_rows,
    tile_cols,
    tile_count,
    neighbor_weight,
    root_weight,
    output_weight,
    cotangent,
):
    node_rows = features.shape[0]
    slice_width = features.shape[1]
    wide_count = lax.axis_size("wide")
    narrow_count = lax.axis_size("narrow")
    tile_side = tile_blocks.shape[-1]
    tile_rows_count = node_rows // tile_side
    group_rows = node_rows // narrow_count
    all_tiles, all_rows, all_cols, all_counts = (
        lax.all_gather(tile_blocks, "narrow", axis=1, tiled=True),
        lax.all_gather(tile_rows, "narrow", axis=1, tiled=True),
        lax.all_gather(tile_cols, "narrow", axis=1, tiled=True),
        lax.all_gather(tile_count, "narrow", axis=1, tiled=True),
    )
    columns = lax.all_gather(features, "wide", axis=0, tiled=True)
    groups = columns.reshape(wide_count, narrow_count, group_rows, slice_width).transpose(
        1, 0, 2, 3
    )
    groups = groups.reshape(narrow_count, -1, tile_side, slice_width)
    running = jnp.zeros((node_rows, slice_width), jnp.float32)
    for source in range(narrow_count):
        running = running + tile_sum(
            all_tiles[0, source],
            all_rows[0, source],
            all_cols[0, source],
            all_counts[0, source],
            groups[source],
            tile_rows_count,
        )
    agg = running.astype(jnp.bfloat16)
    partial_pre = jnp.dot(agg, neighbor_weight, preferred_element_type=jnp.float32) + jnp.dot(
        features, root_weight, preferred_element_type=jnp.float32
    )
    pre = lax.psum(partial_pre, "narrow")
    hidden = jax.nn.silu(pre).astype(jnp.bfloat16)
    narrow_index = lax.axis_index("narrow")
    out_columns = lax.dynamic_slice_in_dim(
        output_weight, narrow_index * slice_width, slice_width, 1
    )
    layer_output = (
        features.astype(jnp.float32)
        + jnp.dot(hidden, out_columns, preferred_element_type=jnp.float32)
    ).astype(jnp.bfloat16)
    hidden_grad = jnp.dot(cotangent, output_weight.T, preferred_element_type=jnp.float32)
    sigmoid_pre = jax.nn.sigmoid(pre)
    pre_grad = (hidden_grad * sigmoid_pre * (1.0 + pre * (1.0 - sigmoid_pre))).astype(jnp.bfloat16)
    cot_columns = lax.dynamic_slice_in_dim(cotangent, narrow_index * slice_width, slice_width, 1)
    neighbor_part = jnp.dot(agg.T, pre_grad, preferred_element_type=jnp.float32)
    root_part = jnp.dot(features.T, pre_grad, preferred_element_type=jnp.float32)
    output_part = jnp.dot(hidden.T, cot_columns, preferred_element_type=jnp.float32)
    neighbor_grad, root_grad, output_grad = lax.psum(
        (neighbor_part, root_part, output_part), "wide"
    )
    return (layer_output, neighbor_grad, root_grad, output_grad)


Y_SIZE = 2
CORES = 2
MESH = pl.DeviceIdType.MESH


def fused_kernel(
    wide, narrow,
    x_hbm, t_hbm, rows_ref, cols_ref, count_hbm, wn_hbm, wr_hbm, ow_hbm, cot_hbm,
    grads_out, lo_out,
    xf, tiles, ow, cot, wn, wr, count_ref, dense, part, hidden_grad, sent, came, pre_all, agg,
    pg, hid, grad32, grad, from_y, to_z, from_z, gall, lo,
    local_sem, send_sem, recv_sem,
):
    z_size = wide // Y_SIZE
    me_b = lax.axis_index("wide")
    me_n = lax.axis_index("narrow")
    z, y = me_b // Y_SIZE, me_b % Y_SIZE
    other_y = 1 - y
    core_n = me_n // CORES * CORES + (1 - me_n % CORES)
    x_n = (me_n + CORES) % narrow
    xc_n = (core_n + CORES) % narrow
    node_rows, width = x_hbm.shape
    hidden_width = ow_hbm.shape[0]
    group = node_rows // narrow
    side = t_hbm.shape[-1]
    slots = t_hbm.shape[2]
    piece = width // wide
    tile_rows_count = node_rows // side
    across = dense.shape[-1] // side
    f32, bf16 = jnp.float32, jnp.bfloat16
    y_dev = (z * Y_SIZE + other_y, me_n)

    def group_rows(n):
        return pl.ds(pl.multiple_of(n * group, group), group)

    def slice_cols(n):
        return pl.ds(pl.multiple_of(n * width, width), width)

    def z_at(dz):
        return lax.rem(z + dz, z_size)

    def z_dev(dz):
        return (z_at(dz) * Y_SIZE + y, me_n)

    def z_source(dz):
        return lax.rem(z + z_size - dz, z_size) * Y_SIZE + y

    used = [0]
    pending = []

    def send(src, dst, device):
        k = used[0]
        used[0] += 1
        copy = pltpu.make_async_remote_copy(
            src_ref=src, dst_ref=dst, send_sem=send_sem.at[k], recv_sem=recv_sem.at[k],
            device_id=device, device_id_type=MESH,
        )
        copy.start()
        pending.append(copy)
        return copy

    barrier = pltpu.get_barrier_semaphore()
    partners = [(me_b, n) for n in (core_n, x_n, xc_n)]
    partners += [z_dev(dz) for dz in range(1, z_size)] + [y_dev]
    for device in partners:
        pl.semaphore_signal(barrier, inc=1, device_id=device, device_id_type=MESH)

    local = [
        pltpu.make_async_copy(src, dst, local_sem.at[k])
        for k, (src, dst) in enumerate(
            (
                (count_hbm, count_ref),
                (t_hbm.at[0, 0], tiles),
                (x_hbm, xf.at[me_b]),
                (wr_hbm, wr),
                (wn_hbm, wn),
                (cot_hbm, cot),
                (ow_hbm, ow),
            )
        )
    ]
    for copy in local:
        copy.start()
    count_copy, tile_copy, x_copy, wr_copy, wn_copy, cot_copy, ow_copy = local

    count_copy.wait()
    live = count_ref[0, 0]
    chunk = 32
    positions = tile_rows_count * across
    steps = side // chunk

    def densify(step):
        at = pl.ds(step * chunk, chunk)

        def add_slot(s, sums):
            tile = tiles[s, at, :].astype(f32)
            place = rows_ref[0, 0, s] * across + cols_ref[0, 0, s]
            place = jnp.where(s < live, place, -1)
            return tuple(
                sums[p] + tile * jnp.where(place == p, 1.0, 0.0).astype(f32)
                for p in range(positions)
            )

        sums = lax.fori_loop(
            0, slots, add_slot,
            tuple(jnp.zeros((chunk, side), f32) for _ in range(positions)),
            unroll=4,
        )
        for p in range(positions):
            dense[me_n, p // across, at, pl.ds(p % across * side, side)] = sums[p].astype(bf16)

    def slab(n, step):
        return dense.at[n, :, pl.ds(step * chunk, chunk), :]

    pl.semaphore_wait(barrier, len(partners))
    z_order = sorted(range(1, z_size), key=lambda dz: abs(dz - z_size / 2))
    x_halves = [pl.ds(h * (node_rows // 2), node_rows // 2) for h in range(2)]
    blocks = {
        (dz, h): send(x_hbm.at[x_halves[h]], xf.at[me_b, x_halves[h]], z_dev(dz))
        for h in range(2)
        for dz in z_order
    }
    y_blocks = [send(x_hbm, xf.at[me_b], y_dev)]
    tile_copy.wait()
    dense_x, dense_core, dense_fwd = [], [], []
    for step in range(steps):
        densify(step)
        dense_x.append(send(slab(me_n, step), slab(me_n, step), (me_b, x_n)))
        dense_core.append(send(slab(me_n, step), slab(me_n, step), (me_b, core_n)))

    def pass_block(dz, h):
        blocks[dz, h].wait_recv()
        part_of = xf.at[z_source(dz), x_halves[h]]
        y_blocks.append(send(part_of, part_of, y_dev))

    def pass_slab(step):
        dense_x[step].wait_recv()
        dense_fwd.append(send(slab(x_n, step), slab(x_n, step), (me_b, core_n)))

    for dz in z_order[1:] + z_order[:1]:
        pass_block(dz, 0)
    for step in range(steps // 2):
        pass_slab(step)
    cot_copy.wait()
    ow_copy.wait()
    hidden_grad[...] = lax.dot_general(
        cot[...], ow[...], (((1,), (1,)), ((), ())), preferred_element_type=f32
    )
    for dz in z_order[1:] + z_order[:1]:
        pass_block(dz, 1)
    for step in range(steps // 2, steps):
        pass_slab(step)
    x_copy.wait()
    wr_copy.wait()
    wn_copy.wait()
    part[...] = jnp.dot(xf[me_b], wr[...], preferred_element_type=f32)

    for copy in y_blocks:
        copy.wait_recv()

    def product(n):
        column_tiles = xf[:, group_rows(n), :].reshape(wide * group, width)
        return jnp.dot(
            dense[n].reshape(node_rows, wide * group), column_tiles, preferred_element_type=f32
        )

    total = product(me_n)
    for copy in dense_core:
        copy.wait_recv()
    total = total + product(core_n)
    total = total + product(x_n)
    for copy in dense_fwd:
        copy.wait_recv()
    total = total + product(xc_n)
    agg[...] = total.astype(bf16)

    def pre_rows(core, q):
        return pl.ds(pl.multiple_of(core * 2 * group + q * group, group), group)

    def gates(rows, pre):
        sig = jax.nn.sigmoid(pre)
        pg[rows, :] = (hidden_grad[rows, :] * sig * (1.0 + pre * (1.0 - sig))).astype(bf16)
        hid[rows, :] = (pre * sig).astype(bf16)

    def half_pre(core):
        rows = pl.ds(pl.multiple_of(core * 2 * group, group), 2 * group)
        return part[rows, :] + jnp.dot(agg[rows, :], wn[...], preferred_element_type=f32)

    my_core = me_n % CORES
    sent[0] = half_pre(1 - my_core).astype(bf16).reshape(2, group, hidden_width)
    to_core = [send(sent.at[0, q], came.at[0, q], (me_b, core_n)) for q in range(2)]
    kept = half_pre(my_core).reshape(2, group, hidden_width)
    kept = [kept[0], kept[1]]
    to_x, back = [], []
    for q in range(2):
        to_core[q].wait_recv()
        kept[q] = kept[q] + came[0, q].astype(f32)
        sent[1, q] = kept[q].astype(bf16)
        to_x.append(send(sent.at[1, q], came.at[1, q], (me_b, x_n)))
    for q in range(2):
        to_x[q].wait_recv()
        pre = kept[q] + came[1, q].astype(f32)
        rows = pre_rows(my_core, q)
        pre_all[rows, :] = pre.astype(bf16)
        back.append(send(pre_all.at[rows, :], pre_all.at[rows, :], (me_b, core_n)))
        gates(rows, pre)
    for q in range(2):
        back[q].wait_recv()
        rows = pre_rows(1 - my_core, q)
        gates(rows, pre_all[rows, :].astype(f32))

    contract_rows = (((0,), (0,)), ((), ()))
    tracks = [pl.ds(k, 1) for k in range(3)]

    def piece_of(track, b):
        return (tracks[track], pl.ds(pl.multiple_of(b * piece, piece), piece), slice(None))

    def fill(k, left, right):
        value = lax.dot_general(left, right, contract_rows, preferred_element_type=f32)
        grad32[k] = value
        grad[k] = value.astype(bf16)

    def to_other_y(track):
        return [
            send(
                grad.at[piece_of(track, z_at(dz) * Y_SIZE + other_y)],
                from_y.at[dz, tracks[track]],
                y_dev,
            )
            for dz in z_order + [0]
        ]

    halves = []
    operands = ((agg[...], pg[...]), (xf[me_b], pg[...]), (cot[:, slice_cols(me_n)], hid[...]))
    for track, (left, right) in enumerate(operands):
        fill(track, left, right)
        halves.append(to_other_y(track))

    sums, arriving_z = [], []
    for track in range(3):
        along = tracks[track]
        arriving_z.append([])
        for dz, copy in zip(z_order + [0], halves[track]):
            copy.wait_recv()
            both = grad32[piece_of(track, z_at(dz) * Y_SIZE + y)] + from_y[dz, along].astype(f32)
            if dz:
                to_z[dz, along] = both.astype(bf16)
                arriving_z[track].append(
                    (dz, send(to_z.at[dz, along], from_z.at[dz, along], z_dev(dz)))
                )
        sums.append(both)
    lo[...] = jnp.dot(hid[...], ow[:, slice_cols(me_n)], preferred_element_type=f32)
    lo_copy = pltpu.make_async_copy(lo, lo_out, local_sem.at[7])
    lo_copy.start()
    last, done = [], []
    for track in range(3):
        both = sums[track]
        for dz, copy in arriving_z[track]:
            copy.wait_recv()
            both = both + from_z[dz, tracks[track]].astype(f32)
        own = piece_of(track, me_b)
        gall[own] = both.astype(bf16)
        done.append({dz: send(gall.at[own], gall.at[own], z_dev(dz)) for dz in z_order})
        last.append(send(gall.at[own], gall.at[own], y_dev))
    for track in range(3):
        for dz in z_order[1:] + z_order[:1]:
            done[track][dz].wait_recv()
            at = piece_of(track, z_source(dz))
            last.append(send(gall.at[at], gall.at[at], y_dev))
    for copy in last:
        copy.wait_recv()
    out_copy = pltpu.make_async_copy(gall, grads_out, local_sem.at[8])
    out_copy.start()
    for copy in pending:
        copy.wait_send()
    lo_copy.wait()
    out_copy.wait()


def finish_kernel(
    x_hbm, product_hbm, grads_hbm, out_hbm, neighbor_hbm, root_hbm, output_hbm,
    x, product, grads, out, neighbor, root, output, in_sem, out_sem,
):
    f32 = jnp.float32
    pairs = [(grads_hbm.at[k], grads.at[k]) for k in (2, 0, 1)]
    pairs += [(x_hbm, x), (product_hbm, product)]
    arriving = [
        pltpu.make_async_copy(src, dst, in_sem.at[k]) for k, (src, dst) in enumerate(pairs)
    ]
    for copy in arriving:
        copy.start()
    leaving = [
        pltpu.make_async_copy(src, dst, out_sem.at[k])
        for k, (src, dst) in enumerate(
            ((output, output_hbm), (neighbor, neighbor_hbm), (root, root_hbm), (out, out_hbm))
        )
    ]
    arriving[0].wait()
    output[...] = grads[2].astype(f32).T
    leaving[0].start()
    arriving[1].wait()
    neighbor[...] = grads[0].astype(f32)
    leaving[1].start()
    arriving[2].wait()
    root[...] = grads[1].astype(f32)
    leaving[2].start()
    arriving[3].wait()
    arriving[4].wait()
    out[...] = (x[...].astype(f32) + product[...]).astype(out.dtype)
    leaving[3].start()
    for copy in leaving:
        copy.wait()


def per_device_fused(
    wide, narrow,
    features, tile_blocks, tile_rows, tile_cols, tile_count,
    neighbor_weight, root_weight, output_weight, cotangent,
):
    node_rows, width = features.shape
    hidden_width = output_weight.shape[0]
    group = node_rows // narrow
    side = tile_blocks.shape[-1]
    z_size = wide // Y_SIZE
    piece = width // wide
    bf16, f32 = jnp.bfloat16, jnp.float32
    copies = 96
    hbm = pl.BlockSpec(memory_space=pltpu.HBM)
    smem = pl.BlockSpec(memory_space=pltpu.SMEM)
    grads, product = pl.pallas_call(
        functools.partial(fused_kernel, wide, narrow),
        out_shape=(
            jax.ShapeDtypeStruct((3, width, hidden_width), bf16),
            jax.ShapeDtypeStruct((node_rows, width), f32),
        ),
        in_specs=[hbm, hbm, smem, smem, hbm, hbm, hbm, hbm, hbm],
        out_specs=(hbm, hbm),
        scratch_shapes=[
            pltpu.VMEM((wide, node_rows, width), bf16),
            pltpu.VMEM(tile_blocks.shape[2:], bf16),
            pltpu.VMEM((hidden_width, hidden_width), bf16),
            pltpu.VMEM((node_rows, hidden_width), bf16),
            pltpu.VMEM((width, hidden_width), bf16),
            pltpu.VMEM((width, hidden_width), bf16),
            pltpu.SMEM(tile_count.shape, jnp.int32),
            pltpu.VMEM((narrow, node_rows // side, side, wide * group), bf16),
            pltpu.VMEM((node_rows, hidden_width), f32),
            pltpu.VMEM((node_rows, hidden_width), f32),
            pltpu.VMEM((2, 2, group, hidden_width), bf16),
            pltpu.VMEM((2, 2, group, hidden_width), bf16),
            pltpu.VMEM((node_rows, hidden_width), bf16),
            pltpu.VMEM((node_rows, width), bf16),
            pltpu.VMEM((node_rows, hidden_width), bf16),
            pltpu.VMEM((node_rows, hidden_width), bf16),
            pltpu.VMEM((3, width, hidden_width), f32),
            pltpu.VMEM((3, width, hidden_width), bf16),
            pltpu.VMEM((z_size, 3, piece, hidden_width), bf16),
            pltpu.VMEM((z_size, 3, piece, hidden_width), bf16),
            pltpu.VMEM((z_size, 3, piece, hidden_width), bf16),
            pltpu.VMEM((3, width, hidden_width), bf16),
            pltpu.VMEM((node_rows, width), f32),
            pltpu.SemaphoreType.DMA((9,)),
            pltpu.SemaphoreType.DMA((copies,)),
            pltpu.SemaphoreType.DMA((copies,)),
        ],
        compiler_params=pltpu.CompilerParams(
            collective_id=0, has_side_effects=True, vmem_limit_bytes=63 * 1024 * 1024
        ),
    )(
        features, tile_blocks, tile_rows, tile_cols, tile_count,
        neighbor_weight, root_weight, output_weight, cotangent,
    )
    return pl.pallas_call(
        finish_kernel,
        out_shape=(
            jax.ShapeDtypeStruct((node_rows, width), bf16),
            jax.ShapeDtypeStruct((width, hidden_width), f32),
            jax.ShapeDtypeStruct((width, hidden_width), f32),
            jax.ShapeDtypeStruct((hidden_width, width), f32),
        ),
        in_specs=[hbm] * 3,
        out_specs=(hbm,) * 4,
        scratch_shapes=[
            pltpu.VMEM((node_rows, width), bf16),
            pltpu.VMEM((node_rows, width), f32),
            pltpu.VMEM((3, width, hidden_width), bf16),
            pltpu.VMEM((node_rows, width), bf16),
            pltpu.VMEM((width, hidden_width), f32),
            pltpu.VMEM((width, hidden_width), f32),
            pltpu.VMEM((hidden_width, width), f32),
            pltpu.SemaphoreType.DMA((5,)),
            pltpu.SemaphoreType.DMA((4,)),
        ],
        compiler_params=pltpu.CompilerParams(vmem_limit_bytes=63 * 1024 * 1024),
    )(features, product, grads)


def solution(mesh):
    wide, narrow = mesh.shape["wide"], mesh.shape["narrow"]
    if wide == 8 and narrow == 4:
        per_device = functools.partial(per_device_fused, wide, narrow)
    else:
        per_device = per_device_large
    return jax.shard_map(
        per_device,
        mesh=mesh,
        in_specs=(
            P("wide", "narrow"),
            P("wide", "narrow", None, None, None),
            P("wide", "narrow", None),
            P("wide", "narrow", None),
            P("wide", "narrow"),
            P("narrow", None),
            P("narrow", None),
            P(),
            P("wide", None),
        ),
        out_specs=(P("wide", "narrow"), P("narrow", None), P("narrow", None), P(None, "narrow")),
        check_vma=False,
    )
```

```python
import functools
import math

import jax
import jax.numpy as jnp
from jax import lax
from jax.experimental import pallas as pl
from jax.experimental.pallas import tpu as pltpu
from jax.sharding import PartitionSpec as P


def tile_sum(block_tiles, row_ids, col_ids, live_count, column_tiles, tile_rows_count):
    capacity = block_tiles.shape[0]
    block_size = math.gcd(capacity, 24)
    tile_side = block_tiles.shape[-1]
    feature_width = column_tiles.shape[-1]
    row_range = jnp.arange(tile_rows_count, dtype=jnp.int32)
    slot_range = jnp.arange(block_size, dtype=jnp.int32)

    def one_turn(turn_index, running):
        first_slot = turn_index * block_size
        some_tiles = lax.dynamic_slice_in_dim(block_tiles, first_slot, block_size, 0)
        some_rows = lax.dynamic_slice_in_dim(row_ids, first_slot, block_size, 0)
        some_cols = lax.dynamic_slice_in_dim(col_ids, first_slot, block_size, 0)
        picked = column_tiles[some_cols]
        product = jnp.einsum("tij,tjh->tih", some_tiles, picked, preferred_element_type=jnp.float32)
        alive = (first_slot + slot_range < live_count).astype(jnp.float32)
        placing = alive[:, None] * (some_rows[:, None] == row_range[None, :]).astype(jnp.float32)
        return running + jnp.einsum("tr,tih->rih", placing, product)

    block_turns = (live_count + block_size - 1) // block_size
    start_value = jnp.zeros((tile_rows_count, tile_side, feature_width), jnp.float32)
    summed = lax.fori_loop(0, block_turns, one_turn, start_value)
    return summed.reshape(tile_rows_count * tile_side, feature_width)


def per_device_large(
    features,
    tile_blocks,
    tile_rows,
    tile_cols,
    tile_count,
    neighbor_weight,
    root_weight,
    output_weight,
    cotangent,
):
    node_rows = features.shape[0]
    slice_width = features.shape[1]
    wide_count = lax.axis_size("wide")
    narrow_count = lax.axis_size("narrow")
    tile_side = tile_blocks.shape[-1]
    tile_rows_count = node_rows // tile_side
    group_rows = node_rows // narrow_count
    all_tiles, all_rows, all_cols, all_counts = (
        lax.all_gather(tile_blocks, "narrow", axis=1, tiled=True),
        lax.all_gather(tile_rows, "narrow", axis=1, tiled=True),
        lax.all_gather(tile_cols, "narrow", axis=1, tiled=True),
        lax.all_gather(tile_count, "narrow", axis=1, tiled=True),
    )
    columns = lax.all_gather(features, "wide", axis=0, tiled=True)
    groups = columns.reshape(wide_count, narrow_count, group_rows, slice_width).transpose(
        1, 0, 2, 3
    )
    groups = groups.reshape(narrow_count, -1, tile_side, slice_width)
    running = jnp.zeros((node_rows, slice_width), jnp.float32)
    for source in range(narrow_count):
        running = running + tile_sum(
            all_tiles[0, source],
            all_rows[0, source],
            all_cols[0, source],
            all_counts[0, source],
            groups[source],
            tile_rows_count,
        )
    agg = running.astype(jnp.bfloat16)
    partial_pre = jnp.dot(agg, neighbor_weight, preferred_element_type=jnp.float32) + jnp.dot(
        features, root_weight, preferred_element_type=jnp.float32
    )
    pre = lax.psum(partial_pre, "narrow")
    hidden = jax.nn.silu(pre).astype(jnp.bfloat16)
    narrow_index = lax.axis_index("narrow")
    out_columns = lax.dynamic_slice_in_dim(
        output_weight, narrow_index * slice_width, slice_width, 1
    )
    layer_output = (
        features.astype(jnp.float32)
        + jnp.dot(hidden, out_columns, preferred_element_type=jnp.float32)
    ).astype(jnp.bfloat16)
    hidden_grad = jnp.dot(cotangent, output_weight.T, preferred_element_type=jnp.float32)
    sigmoid_pre = jax.nn.sigmoid(pre)
    pre_grad = (hidden_grad * sigmoid_pre * (1.0 + pre * (1.0 - sigmoid_pre))).astype(jnp.bfloat16)
    cot_columns = lax.dynamic_slice_in_dim(cotangent, narrow_index * slice_width, slice_width, 1)
    neighbor_part = jnp.dot(agg.T, pre_grad, preferred_element_type=jnp.float32)
    root_part = jnp.dot(features.T, pre_grad, preferred_element_type=jnp.float32)
    output_part = jnp.dot(hidden.T, cot_columns, preferred_element_type=jnp.float32)
    neighbor_grad, root_grad, output_grad = lax.psum(
        (neighbor_part, root_part, output_part), "wide"
    )
    return (layer_output, neighbor_grad, root_grad, output_grad)


Y_SIZE = 2
CORES = 2
MESH = pl.DeviceIdType.MESH


def fused_kernel(
    wide, narrow,
    x_hbm, t_hbm, rows_ref, cols_ref, count_hbm, wn_hbm, wr_hbm, ow_hbm, cot_hbm,
    grads_out, lo_out,
    xf, tiles, ow, cot, wn, wr, count_ref, dense, part, hidden_grad, sent, came, pre_all, agg,
    pg, hid, grad32, grad, from_y, to_z, from_z, gall, lo,
    local_sem, send_sem, recv_sem,
):
    z_size = wide // Y_SIZE
    me_b = lax.axis_index("wide")
    me_n = lax.axis_index("narrow")
    z, y = me_b // Y_SIZE, me_b % Y_SIZE
    other_y = 1 - y
    core_n = me_n // CORES * CORES + (1 - me_n % CORES)
    x_n = (me_n + CORES) % narrow
    xc_n = (core_n + CORES) % narrow
    node_rows, width = x_hbm.shape
    hidden_width = ow_hbm.shape[0]
    group = node_rows // narrow
    side = t_hbm.shape[-1]
    slots = t_hbm.shape[2]
    piece = width // wide
    tile_rows_count = node_rows // side
    across = dense.shape[-1] // side
    f32, bf16 = jnp.float32, jnp.bfloat16
    y_dev = (z * Y_SIZE + other_y, me_n)

    def group_rows(n):
        return pl.ds(pl.multiple_of(n * group, group), group)

    def slice_cols(n):
        return pl.ds(pl.multiple_of(n * width, width), width)

    def z_at(dz):
        return lax.rem(z + dz, z_size)

    def z_dev(dz):
        return (z_at(dz) * Y_SIZE + y, me_n)

    def z_source(dz):
        return lax.rem(z + z_size - dz, z_size) * Y_SIZE + y

    used = [0]
    pending = []

    def send(src, dst, device):
        k = used[0]
        used[0] += 1
        copy = pltpu.make_async_remote_copy(
            src_ref=src, dst_ref=dst, send_sem=send_sem.at[k], recv_sem=recv_sem.at[k],
            device_id=device, device_id_type=MESH,
        )
        copy.start()
        pending.append(copy)
        return copy

    barrier = pltpu.get_barrier_semaphore()
    partners = [(me_b, n) for n in (core_n, x_n, xc_n)]
    partners += [z_dev(dz) for dz in range(1, z_size)] + [y_dev]
    for device in partners:
        pl.semaphore_signal(barrier, inc=1, device_id=device, device_id_type=MESH)

    local = [
        pltpu.make_async_copy(src, dst, local_sem.at[k])
        for k, (src, dst) in enumerate(
            (
                (count_hbm, count_ref),
                (t_hbm.at[0, 0], tiles),
                (x_hbm, xf.at[me_b]),
                (wr_hbm, wr),
                (wn_hbm, wn),
                (cot_hbm, cot),
                (ow_hbm, ow),
            )
        )
    ]
    for copy in local:
        copy.start()
    count_copy, tile_copy, x_copy, wr_copy, wn_copy, cot_copy, ow_copy = local

    count_copy.wait()
    live = count_ref[0, 0]
    chunk = 32
    positions = tile_rows_count * across
    steps = side // chunk

    def densify(step):
        at = pl.ds(step * chunk, chunk)

        def add_slot(s, sums):
            tile = tiles[s, at, :].astype(f32)
            place = rows_ref[0, 0, s] * across + cols_ref[0, 0, s]
            place = jnp.where(s < live, place, -1)
            return tuple(
                sums[p] + tile * jnp.where(place == p, 1.0, 0.0).astype(f32)
                for p in range(positions)
            )

        sums = lax.fori_loop(
            0, slots, add_slot,
            tuple(jnp.zeros((chunk, side), f32) for _ in range(positions)),
            unroll=4,
        )
        for p in range(positions):
            dense[me_n, p // across, at, pl.ds(p % across * side, side)] = sums[p].astype(bf16)

    def slab(n, step):
        return dense.at[n, :, pl.ds(step * chunk, chunk), :]

    pl.semaphore_wait(barrier, len(partners))
    z_order = sorted(range(1, z_size), key=lambda dz: abs(dz - z_size / 2))
    x_halves = [pl.ds(h * (node_rows // 2), node_rows // 2) for h in range(2)]
    blocks = {
        (dz, h): send(x_hbm.at[x_halves[h]], xf.at[me_b, x_halves[h]], z_dev(dz))
        for h in range(2)
        for dz in z_order
    }
    y_blocks = [send(x_hbm, xf.at[me_b], y_dev)]
    tile_copy.wait()
    dense_x, dense_core, dense_fwd = [], [], []
    for step in range(steps):
        densify(step)
        dense_x.append(send(slab(me_n, step), slab(me_n, step), (me_b, x_n)))
        dense_core.append(send(slab(me_n, step), slab(me_n, step), (me_b, core_n)))

    def pass_block(dz, h):
        blocks[dz, h].wait_recv()
        part_of = xf.at[z_source(dz), x_halves[h]]
        y_blocks.append(send(part_of, part_of, y_dev))

    def pass_slab(step):
        dense_x[step].wait_recv()
        dense_fwd.append(send(slab(x_n, step), slab(x_n, step), (me_b, core_n)))

    for dz in z_order[1:] + z_order[:1]:
        pass_block(dz, 0)
    for step in range(steps // 2):
        pass_slab(step)
    cot_copy.wait()
    ow_copy.wait()
    hidden_grad[...] = lax.dot_general(
        cot[...], ow[...], (((1,), (1,)), ((), ())), preferred_element_type=f32
    )
    for dz in z_order[1:] + z_order[:1]:
        pass_block(dz, 1)
    for step in range(steps // 2, steps):
        pass_slab(step)
    x_copy.wait()
    wr_copy.wait()
    wn_copy.wait()
    part[...] = jnp.dot(xf[me_b], wr[...], preferred_element_type=f32)

    for copy in y_blocks:
        copy.wait_recv()

    def product(n):
        column_tiles = xf[:, group_rows(n), :].reshape(wide * group, width)
        return jnp.dot(
            dense[n].reshape(node_rows, wide * group), column_tiles, preferred_element_type=f32
        )

    total = product(me_n)
    for copy in dense_core:
        copy.wait_recv()
    total = total + product(core_n)
    total = total + product(x_n)
    for copy in dense_fwd:
        copy.wait_recv()
    total = total + product(xc_n)
    agg[...] = total.astype(bf16)

    def pre_rows(core, q):
        return pl.ds(pl.multiple_of(core * 2 * group + q * group, group), group)

    def gates(rows, pre):
        sig = jax.nn.sigmoid(pre)
        pg[rows, :] = (hidden_grad[rows, :] * sig * (1.0 + pre * (1.0 - sig))).astype(bf16)
        hid[rows, :] = (pre * sig).astype(bf16)

    def half_pre(core):
        rows = pl.ds(pl.multiple_of(core * 2 * group, group), 2 * group)
        return part[rows, :] + jnp.dot(agg[rows, :], wn[...], preferred_element_type=f32)

    my_core = me_n % CORES
    sent[0] = half_pre(1 - my_core).astype(bf16).reshape(2, group, hidden_width)
    to_core = [send(sent.at[0, q], came.at[0, q], (me_b, core_n)) for q in range(2)]
    kept = half_pre(my_core).reshape(2, group, hidden_width)
    kept = [kept[0], kept[1]]
    to_x, back = [], []
    for q in range(2):
        to_core[q].wait_recv()
        kept[q] = kept[q] + came[0, q].astype(f32)
        sent[1, q] = kept[q].astype(bf16)
        to_x.append(send(sent.at[1, q], came.at[1, q], (me_b, x_n)))
    for q in range(2):
        to_x[q].wait_recv()
        pre = kept[q] + came[1, q].astype(f32)
        rows = pre_rows(my_core, q)
        pre_all[rows, :] = pre.astype(bf16)
        back.append(send(pre_all.at[rows, :], pre_all.at[rows, :], (me_b, core_n)))
        gates(rows, pre)
    for q in range(2):
        back[q].wait_recv()
        rows = pre_rows(1 - my_core, q)
        gates(rows, pre_all[rows, :].astype(f32))

    contract_rows = (((0,), (0,)), ((), ()))
    tracks = [pl.ds(0, 3)]

    def piece_of(track, b):
        return (tracks[track], pl.ds(pl.multiple_of(b * piece, piece), piece), slice(None))

    def fill(k, left, right):
        value = lax.dot_general(left, right, contract_rows, preferred_element_type=f32)
        grad32[k] = value
        grad[k] = value.astype(bf16)

    def to_other_y(track):
        return [
            send(
                grad.at[piece_of(track, z_at(dz) * Y_SIZE + other_y)],
                from_y.at[dz, tracks[track]],
                y_dev,
            )
            for dz in z_order + [0]
        ]

    halves = []
    operands = ((agg[...], pg[...]), (xf[me_b], pg[...]), (cot[:, slice_cols(me_n)], hid[...]))
    for k, (left, right) in enumerate(operands):
        fill(k, left, right)
    halves.append(to_other_y(0))

    sums, arriving_z = [], []
    for track in range(1):
        along = tracks[track]
        arriving_z.append([])
        for dz, copy in zip(z_order + [0], halves[track]):
            copy.wait_recv()
            both = grad32[piece_of(track, z_at(dz) * Y_SIZE + y)] + from_y[dz, along].astype(f32)
            if dz:
                to_z[dz, along] = both.astype(bf16)
                arriving_z[track].append(
                    (dz, send(to_z.at[dz, along], from_z.at[dz, along], z_dev(dz)))
                )
        sums.append(both)
    lo[...] = jnp.dot(hid[...], ow[:, slice_cols(me_n)], preferred_element_type=f32)
    lo_copy = pltpu.make_async_copy(lo, lo_out, local_sem.at[7])
    lo_copy.start()
    last, done = [], []
    for track in range(1):
        both = sums[track]
        for dz, copy in arriving_z[track]:
            copy.wait_recv()
            both = both + from_z[dz, tracks[track]].astype(f32)
        own = piece_of(track, me_b)
        gall[own] = both.astype(bf16)
        done.append({dz: send(gall.at[own], gall.at[own], z_dev(dz)) for dz in z_order})
        last.append(send(gall.at[own], gall.at[own], y_dev))
    for track in range(1):
        for dz in z_order[1:] + z_order[:1]:
            done[track][dz].wait_recv()
            at = piece_of(track, z_source(dz))
            last.append(send(gall.at[at], gall.at[at], y_dev))
    for copy in last:
        copy.wait_recv()
    out_copy = pltpu.make_async_copy(gall, grads_out, local_sem.at[8])
    out_copy.start()
    for copy in pending:
        copy.wait_send()
    lo_copy.wait()
    out_copy.wait()


def finish_kernel(
    x_hbm, product_hbm, grads_hbm, out_hbm, neighbor_hbm, root_hbm, output_hbm,
    x, product, grads, out, neighbor, root, output, in_sem, out_sem,
):
    f32 = jnp.float32
    pairs = [(grads_hbm.at[k], grads.at[k]) for k in (2, 0, 1)]
    pairs += [(x_hbm, x), (product_hbm, product)]
    arriving = [
        pltpu.make_async_copy(src, dst, in_sem.at[k]) for k, (src, dst) in enumerate(pairs)
    ]
    for copy in arriving:
        copy.start()
    leaving = [
        pltpu.make_async_copy(src, dst, out_sem.at[k])
        for k, (src, dst) in enumerate(
            ((output, output_hbm), (neighbor, neighbor_hbm), (root, root_hbm), (out, out_hbm))
        )
    ]
    arriving[0].wait()
    output[...] = grads[2].astype(f32).T
    leaving[0].start()
    arriving[1].wait()
    neighbor[...] = grads[0].astype(f32)
    leaving[1].start()
    arriving[2].wait()
    root[...] = grads[1].astype(f32)
    leaving[2].start()
    arriving[3].wait()
    arriving[4].wait()
    out[...] = (x[...].astype(f32) + product[...]).astype(out.dtype)
    leaving[3].start()
    for copy in leaving:
        copy.wait()


def per_device_fused(
    wide, narrow,
    features, tile_blocks, tile_rows, tile_cols, tile_count,
    neighbor_weight, root_weight, output_weight, cotangent,
):
    node_rows, width = features.shape
    hidden_width = output_weight.shape[0]
    group = node_rows // narrow
    side = tile_blocks.shape[-1]
    z_size = wide // Y_SIZE
    piece = width // wide
    bf16, f32 = jnp.bfloat16, jnp.float32
    copies = 96
    hbm = pl.BlockSpec(memory_space=pltpu.HBM)
    smem = pl.BlockSpec(memory_space=pltpu.SMEM)
    grads, product = pl.pallas_call(
        functools.partial(fused_kernel, wide, narrow),
        out_shape=(
            jax.ShapeDtypeStruct((3, width, hidden_width), bf16),
            jax.ShapeDtypeStruct((node_rows, width), f32),
        ),
        in_specs=[hbm, hbm, smem, smem, hbm, hbm, hbm, hbm, hbm],
        out_specs=(hbm, hbm),
        scratch_shapes=[
            pltpu.VMEM((wide, node_rows, width), bf16),
            pltpu.VMEM(tile_blocks.shape[2:], bf16),
            pltpu.VMEM((hidden_width, hidden_width), bf16),
            pltpu.VMEM((node_rows, hidden_width), bf16),
            pltpu.VMEM((width, hidden_width), bf16),
            pltpu.VMEM((width, hidden_width), bf16),
            pltpu.SMEM(tile_count.shape, jnp.int32),
            pltpu.VMEM((narrow, node_rows // side, side, wide * group), bf16),
            pltpu.VMEM((node_rows, hidden_width), f32),
            pltpu.VMEM((node_rows, hidden_width), f32),
            pltpu.VMEM((2, 2, group, hidden_width), bf16),
            pltpu.VMEM((2, 2, group, hidden_width), bf16),
            pltpu.VMEM((node_rows, hidden_width), bf16),
            pltpu.VMEM((node_rows, width), bf16),
            pltpu.VMEM((node_rows, hidden_width), bf16),
            pltpu.VMEM((node_rows, hidden_width), bf16),
            pltpu.VMEM((3, width, hidden_width), f32),
            pltpu.VMEM((3, width, hidden_width), bf16),
            pltpu.VMEM((z_size, 3, piece, hidden_width), bf16),
            pltpu.VMEM((z_size, 3, piece, hidden_width), bf16),
            pltpu.VMEM((z_size, 3, piece, hidden_width), bf16),
            pltpu.VMEM((3, width, hidden_width), bf16),
            pltpu.VMEM((node_rows, width), f32),
            pltpu.SemaphoreType.DMA((9,)),
            pltpu.SemaphoreType.DMA((copies,)),
            pltpu.SemaphoreType.DMA((copies,)),
        ],
        compiler_params=pltpu.CompilerParams(
            collective_id=0, has_side_effects=True, vmem_limit_bytes=63 * 1024 * 1024
        ),
    )(
        features, tile_blocks, tile_rows, tile_cols, tile_count,
        neighbor_weight, root_weight, output_weight, cotangent,
    )
    return pl.pallas_call(
        finish_kernel,
        out_shape=(
            jax.ShapeDtypeStruct((node_rows, width), bf16),
            jax.ShapeDtypeStruct((width, hidden_width), f32),
            jax.ShapeDtypeStruct((width, hidden_width), f32),
            jax.ShapeDtypeStruct((hidden_width, width), f32),
        ),
        in_specs=[hbm] * 3,
        out_specs=(hbm,) * 4,
        scratch_shapes=[
            pltpu.VMEM((node_rows, width), bf16),
            pltpu.VMEM((node_rows, width), f32),
            pltpu.VMEM((3, width, hidden_width), bf16),
            pltpu.VMEM((node_rows, width), bf16),
            pltpu.VMEM((width, hidden_width), f32),
            pltpu.VMEM((width, hidden_width), f32),
            pltpu.VMEM((hidden_width, width), f32),
            pltpu.SemaphoreType.DMA((5,)),
            pltpu.SemaphoreType.DMA((4,)),
        ],
        compiler_params=pltpu.CompilerParams(vmem_limit_bytes=63 * 1024 * 1024),
    )(features, product, grads)


def solution(mesh):
    wide, narrow = mesh.shape["wide"], mesh.shape["narrow"]
    if wide == 8 and narrow == 4:
        per_device = functools.partial(per_device_fused, wide, narrow)
    else:
        per_device = per_device_large
    return jax.shard_map(
        per_device,
        mesh=mesh,
        in_specs=(
            P("wide", "narrow"),
            P("wide", "narrow", None, None, None),
            P("wide", "narrow", None),
            P("wide", "narrow", None),
            P("wide", "narrow"),
            P("narrow", None),
            P("narrow", None),
            P(),
            P("wide", None),
        ),
        out_specs=(P("wide", "narrow"), P("narrow", None), P("narrow", None), P(None, "narrow")),
        check_vma=False,
    )
```

```python
import functools
import math

import jax
import jax.numpy as jnp
from jax import lax
from jax.experimental import pallas as pl
from jax.experimental.pallas import tpu as pltpu
from jax.sharding import PartitionSpec as P


def tile_sum(block_tiles, row_ids, col_ids, live_count, column_tiles, tile_rows_count):
    capacity = block_tiles.shape[0]
    block_size = math.gcd(capacity, 24)
    tile_side = block_tiles.shape[-1]
    feature_width = column_tiles.shape[-1]
    row_range = jnp.arange(tile_rows_count, dtype=jnp.int32)
    slot_range = jnp.arange(block_size, dtype=jnp.int32)

    def one_turn(turn_index, running):
        first_slot = turn_index * block_size
        some_tiles = lax.dynamic_slice_in_dim(block_tiles, first_slot, block_size, 0)
        some_rows = lax.dynamic_slice_in_dim(row_ids, first_slot, block_size, 0)
        some_cols = lax.dynamic_slice_in_dim(col_ids, first_slot, block_size, 0)
        picked = column_tiles[some_cols]
        product = jnp.einsum("tij,tjh->tih", some_tiles, picked, preferred_element_type=jnp.float32)
        alive = (first_slot + slot_range < live_count).astype(jnp.float32)
        placing = alive[:, None] * (some_rows[:, None] == row_range[None, :]).astype(jnp.float32)
        return running + jnp.einsum("tr,tih->rih", placing, product)

    block_turns = (live_count + block_size - 1) // block_size
    start_value = jnp.zeros((tile_rows_count, tile_side, feature_width), jnp.float32)
    summed = lax.fori_loop(0, block_turns, one_turn, start_value)
    return summed.reshape(tile_rows_count * tile_side, feature_width)


def per_device_large(
    features,
    tile_blocks,
    tile_rows,
    tile_cols,
    tile_count,
    neighbor_weight,
    root_weight,
    output_weight,
    cotangent,
):
    node_rows = features.shape[0]
    slice_width = features.shape[1]
    wide_count = lax.axis_size("wide")
    narrow_count = lax.axis_size("narrow")
    tile_side = tile_blocks.shape[-1]
    tile_rows_count = node_rows // tile_side
    group_rows = node_rows // narrow_count
    all_tiles, all_rows, all_cols, all_counts = (
        lax.all_gather(tile_blocks, "narrow", axis=1, tiled=True),
        lax.all_gather(tile_rows, "narrow", axis=1, tiled=True),
        lax.all_gather(tile_cols, "narrow", axis=1, tiled=True),
        lax.all_gather(tile_count, "narrow", axis=1, tiled=True),
    )
    columns = lax.all_gather(features, "wide", axis=0, tiled=True)
    groups = columns.reshape(wide_count, narrow_count, group_rows, slice_width).transpose(
        1, 0, 2, 3
    )
    groups = groups.reshape(narrow_count, -1, tile_side, slice_width)
    running = jnp.zeros((node_rows, slice_width), jnp.float32)
    for source in range(narrow_count):
        running = running + tile_sum(
            all_tiles[0, source],
            all_rows[0, source],
            all_cols[0, source],
            all_counts[0, source],
            groups[source],
            tile_rows_count,
        )
    agg = running.astype(jnp.bfloat16)
    partial_pre = jnp.dot(agg, neighbor_weight, preferred_element_type=jnp.float32) + jnp.dot(
        features, root_weight, preferred_element_type=jnp.float32
    )
    pre = lax.psum(partial_pre, "narrow")
    hidden = jax.nn.silu(pre).astype(jnp.bfloat16)
    narrow_index = lax.axis_index("narrow")
    out_columns = lax.dynamic_slice_in_dim(
        output_weight, narrow_index * slice_width, slice_width, 1
    )
    layer_output = (
        features.astype(jnp.float32)
        + jnp.dot(hidden, out_columns, preferred_element_type=jnp.float32)
    ).astype(jnp.bfloat16)
    hidden_grad = jnp.dot(cotangent, output_weight.T, preferred_element_type=jnp.float32)
    sigmoid_pre = jax.nn.sigmoid(pre)
    pre_grad = (hidden_grad * sigmoid_pre * (1.0 + pre * (1.0 - sigmoid_pre))).astype(jnp.bfloat16)
    cot_columns = lax.dynamic_slice_in_dim(cotangent, narrow_index * slice_width, slice_width, 1)
    neighbor_part = jnp.dot(agg.T, pre_grad, preferred_element_type=jnp.float32)
    root_part = jnp.dot(features.T, pre_grad, preferred_element_type=jnp.float32)
    output_part = jnp.dot(hidden.T, cot_columns, preferred_element_type=jnp.float32)
    neighbor_grad, root_grad, output_grad = lax.psum(
        (neighbor_part, root_part, output_part), "wide"
    )
    return (layer_output, neighbor_grad, root_grad, output_grad)


Y_SIZE = 2
CORES = 2
MESH = pl.DeviceIdType.MESH


def fused_kernel(
    wide, narrow,
    x_hbm, t_hbm, rows_ref, cols_ref, count_hbm, wn_hbm, wr_hbm, ow_hbm, cot_hbm,
    grads_out, lo_out,
    xf, tiles, ow, cot, wn, wr, count_ref, dense, part, hidden_grad, sent, came, pre_all, agg,
    pg, hid, grad32, grad, from_y, to_z, from_z, gall, lo,
    local_sem, send_sem, recv_sem,
):
    z_size = wide // Y_SIZE
    me_b = lax.axis_index("wide")
    me_n = lax.axis_index("narrow")
    z, y = me_b // Y_SIZE, me_b % Y_SIZE
    other_y = 1 - y
    core_n = me_n // CORES * CORES + (1 - me_n % CORES)
    x_n = (me_n + CORES) % narrow
    xc_n = (core_n + CORES) % narrow
    node_rows, width = x_hbm.shape
    hidden_width = ow_hbm.shape[0]
    group = node_rows // narrow
    side = t_hbm.shape[-1]
    slots = t_hbm.shape[2]
    piece = width // wide
    tile_rows_count = node_rows // side
    across = dense.shape[-1] // side
    f32, bf16 = jnp.float32, jnp.bfloat16
    y_dev = (z * Y_SIZE + other_y, me_n)

    def group_rows(n):
        return pl.ds(pl.multiple_of(n * group, group), group)

    def slice_cols(n):
        return pl.ds(pl.multiple_of(n * width, width), width)

    def z_at(dz):
        return lax.rem(z + dz, z_size)

    def z_dev(dz):
        return (z_at(dz) * Y_SIZE + y, me_n)

    def z_source(dz):
        return lax.rem(z + z_size - dz, z_size) * Y_SIZE + y

    used = [0]
    pending = []

    def send(src, dst, device):
        k = used[0]
        used[0] += 1
        copy = pltpu.make_async_remote_copy(
            src_ref=src, dst_ref=dst, send_sem=send_sem.at[k], recv_sem=recv_sem.at[k],
            device_id=device, device_id_type=MESH,
        )
        copy.start()
        pending.append(copy)
        return copy

    barrier = pltpu.get_barrier_semaphore()
    partners = [(me_b, n) for n in (core_n, x_n, xc_n)]
    partners += [z_dev(dz) for dz in range(1, z_size)] + [y_dev]
    for device in partners:
        pl.semaphore_signal(barrier, inc=1, device_id=device, device_id_type=MESH)

    local = [
        pltpu.make_async_copy(src, dst, local_sem.at[k])
        for k, (src, dst) in enumerate(
            (
                (count_hbm, count_ref),
                (t_hbm.at[0, 0], tiles),
                (x_hbm, xf.at[me_b]),
                (wr_hbm, wr),
                (wn_hbm, wn),
                (cot_hbm, cot),
                (ow_hbm, ow),
            )
        )
    ]
    for copy in local:
        copy.start()
    count_copy, tile_copy, x_copy, wr_copy, wn_copy, cot_copy, ow_copy = local

    count_copy.wait()
    live = count_ref[0, 0]
    chunk = 32
    positions = tile_rows_count * across
    steps = side // chunk

    def densify(step):
        at = pl.ds(step * chunk, chunk)

        def add_slot(s, sums):
            tile = tiles[s, at, :].astype(f32)
            place = rows_ref[0, 0, s] * across + cols_ref[0, 0, s]
            place = jnp.where(s < live, place, -1)
            return tuple(
                sums[p] + tile * jnp.where(place == p, 1.0, 0.0).astype(f32)
                for p in range(positions)
            )

        sums = lax.fori_loop(
            0, slots, add_slot,
            tuple(jnp.zeros((chunk, side), f32) for _ in range(positions)),
            unroll=4,
        )
        for p in range(positions):
            dense[me_n, p // across, at, pl.ds(p % across * side, side)] = sums[p].astype(bf16)

    def slab(n, step):
        return dense.at[n, :, pl.ds(step * chunk, chunk), :]

    pl.semaphore_wait(barrier, len(partners))
    z_order = sorted(range(1, z_size), key=lambda dz: abs(dz - z_size / 2))
    x_halves = [pl.ds(h * (node_rows // 2), node_rows // 2) for h in range(2)]
    blocks = {
        (dz, h): send(x_hbm.at[x_halves[h]], xf.at[me_b, x_halves[h]], z_dev(dz))
        for h in range(2)
        for dz in z_order
    }
    y_blocks = [send(x_hbm, xf.at[me_b], y_dev)]
    tile_copy.wait()
    dense_x, dense_core, dense_fwd = [], [], []
    for step in range(steps):
        densify(step)
        dense_x.append(send(slab(me_n, step), slab(me_n, step), (me_b, x_n)))
        dense_core.append(send(slab(me_n, step), slab(me_n, step), (me_b, core_n)))

    def pass_block(dz, h):
        blocks[dz, h].wait_recv()
        part_of = xf.at[z_source(dz), x_halves[h]]
        y_blocks.append(send(part_of, part_of, y_dev))

    def pass_slab(step):
        dense_x[step].wait_recv()
        dense_fwd.append(send(slab(x_n, step), slab(x_n, step), (me_b, core_n)))

    for dz in z_order[1:] + z_order[:1]:
        pass_block(dz, 0)
    for step in range(steps // 2):
        pass_slab(step)
    for dz in z_order[1:] + z_order[:1]:
        pass_block(dz, 1)
    for step in range(steps // 2, steps):
        pass_slab(step)
    x_copy.wait()
    wr_copy.wait()
    wn_copy.wait()
    part[...] = jnp.dot(xf[me_b], wr[...], preferred_element_type=f32)

    for copy in y_blocks:
        copy.wait_recv()

    def product(n):
        column_tiles = xf[:, group_rows(n), :].reshape(wide * group, width)
        return jnp.dot(
            dense[n].reshape(node_rows, wide * group), column_tiles, preferred_element_type=f32
        )

    total = product(me_n)
    for copy in dense_core:
        copy.wait_recv()
    total = total + product(core_n)
    total = total + product(x_n)
    for copy in dense_fwd:
        copy.wait_recv()
    total = total + product(xc_n)
    agg[...] = total.astype(bf16)

    def pre_rows(core, q):
        return pl.ds(pl.multiple_of(core * 2 * group + q * group, group), group)

    def gates(rows, pre):
        sig = jax.nn.sigmoid(pre)
        pg[rows, :] = (hidden_grad[rows, :] * sig * (1.0 + pre * (1.0 - sig))).astype(bf16)
        hid[rows, :] = (pre * sig).astype(bf16)

    def half_pre(core):
        rows = pl.ds(pl.multiple_of(core * 2 * group, group), 2 * group)
        return part[rows, :] + jnp.dot(agg[rows, :], wn[...], preferred_element_type=f32)

    my_core = me_n % CORES
    sent[0] = half_pre(1 - my_core).astype(bf16).reshape(2, group, hidden_width)
    to_core = [send(sent.at[0, q], came.at[0, q], (me_b, core_n)) for q in range(2)]
    kept = half_pre(my_core).reshape(2, group, hidden_width)
    kept = [kept[0], kept[1]]
    to_x, back = [], []
    for q in range(2):
        to_core[q].wait_recv()
        kept[q] = kept[q] + came[0, q].astype(f32)
        sent[1, q] = kept[q].astype(bf16)
        to_x.append(send(sent.at[1, q], came.at[1, q], (me_b, x_n)))
    cot_copy.wait()
    ow_copy.wait()
    hidden_grad[...] = lax.dot_general(
        cot[...], ow[...], (((1,), (1,)), ((), ())), preferred_element_type=f32
    )
    for q in range(2):
        to_x[q].wait_recv()
        pre = kept[q] + came[1, q].astype(f32)
        rows = pre_rows(my_core, q)
        pre_all[rows, :] = pre.astype(bf16)
        back.append(send(pre_all.at[rows, :], pre_all.at[rows, :], (me_b, core_n)))
        gates(rows, pre)
    for q in range(2):
        back[q].wait_recv()
        rows = pre_rows(1 - my_core, q)
        gates(rows, pre_all[rows, :].astype(f32))

    contract_rows = (((0,), (0,)), ((), ()))
    tracks = (pl.ds(0, 2), pl.ds(2, 1))

    def piece_of(track, b):
        return (tracks[track], pl.ds(pl.multiple_of(b * piece, piece), piece), slice(None))

    def fill(k, left, right):
        value = lax.dot_general(left, right, contract_rows, preferred_element_type=f32)
        grad32[k] = value
        grad[k] = value.astype(bf16)

    def to_other_y(track):
        return [
            send(
                grad.at[piece_of(track, z_at(dz) * Y_SIZE + other_y)],
                from_y.at[dz, tracks[track]],
                y_dev,
            )
            for dz in z_order + [0]
        ]

    halves = []
    operands = ((agg[...], pg[...]), (xf[me_b], pg[...]), (cot[:, slice_cols(me_n)], hid[...]))
    for k, (left, right) in enumerate(operands):
        fill(k, left, right)
        if k:
            halves.append(to_other_y(k - 1))

    sums, arriving_z = [], []
    for track in range(2):
        along = tracks[track]
        arriving_z.append([])
        for dz, copy in zip(z_order + [0], halves[track]):
            copy.wait_recv()
            both = grad32[piece_of(track, z_at(dz) * Y_SIZE + y)] + from_y[dz, along].astype(f32)
            if dz:
                to_z[dz, along] = both.astype(bf16)
                arriving_z[track].append(
                    (dz, send(to_z.at[dz, along], from_z.at[dz, along], z_dev(dz)))
                )
        sums.append(both)
    lo[...] = jnp.dot(hid[...], ow[:, slice_cols(me_n)], preferred_element_type=f32)
    lo_copy = pltpu.make_async_copy(lo, lo_out, local_sem.at[7])
    lo_copy.start()
    last, done = [], []
    for track in range(2):
        both = sums[track]
        for dz, copy in arriving_z[track]:
            copy.wait_recv()
            both = both + from_z[dz, tracks[track]].astype(f32)
        own = piece_of(track, me_b)
        gall[own] = both.astype(bf16)
        done.append({dz: send(gall.at[own], gall.at[own], z_dev(dz)) for dz in z_order})
        last.append(send(gall.at[own], gall.at[own], y_dev))
    for track in range(2):
        for dz in z_order[1:] + z_order[:1]:
            done[track][dz].wait_recv()
            at = piece_of(track, z_source(dz))
            last.append(send(gall.at[at], gall.at[at], y_dev))
    for copy in last:
        copy.wait_recv()
    out_copy = pltpu.make_async_copy(gall, grads_out, local_sem.at[8])
    out_copy.start()
    for copy in pending:
        copy.wait_send()
    lo_copy.wait()
    out_copy.wait()


def finish_kernel(
    x_hbm, product_hbm, grads_hbm, out_hbm, neighbor_hbm, root_hbm, output_hbm,
    x, product, grads, out, neighbor, root, output, in_sem, out_sem,
):
    f32 = jnp.float32
    pairs = [(grads_hbm.at[k], grads.at[k]) for k in (2, 0, 1)]
    pairs += [(x_hbm, x), (product_hbm, product)]
    arriving = [
        pltpu.make_async_copy(src, dst, in_sem.at[k]) for k, (src, dst) in enumerate(pairs)
    ]
    for copy in arriving:
        copy.start()
    leaving = [
        pltpu.make_async_copy(src, dst, out_sem.at[k])
        for k, (src, dst) in enumerate(
            ((output, output_hbm), (neighbor, neighbor_hbm), (root, root_hbm), (out, out_hbm))
        )
    ]
    arriving[0].wait()
    output[...] = grads[2].astype(f32).T
    leaving[0].start()
    arriving[1].wait()
    neighbor[...] = grads[0].astype(f32)
    leaving[1].start()
    arriving[2].wait()
    root[...] = grads[1].astype(f32)
    leaving[2].start()
    arriving[3].wait()
    arriving[4].wait()
    out[...] = (x[...].astype(f32) + product[...]).astype(out.dtype)
    leaving[3].start()
    for copy in leaving:
        copy.wait()


def per_device_fused(
    wide, narrow,
    features, tile_blocks, tile_rows, tile_cols, tile_count,
    neighbor_weight, root_weight, output_weight, cotangent,
):
    node_rows, width = features.shape
    hidden_width = output_weight.shape[0]
    group = node_rows // narrow
    side = tile_blocks.shape[-1]
    z_size = wide // Y_SIZE
    piece = width // wide
    bf16, f32 = jnp.bfloat16, jnp.float32
    copies = 96
    hbm = pl.BlockSpec(memory_space=pltpu.HBM)
    smem = pl.BlockSpec(memory_space=pltpu.SMEM)
    grads, product = pl.pallas_call(
        functools.partial(fused_kernel, wide, narrow),
        out_shape=(
            jax.ShapeDtypeStruct((3, width, hidden_width), bf16),
            jax.ShapeDtypeStruct((node_rows, width), f32),
        ),
        in_specs=[hbm, hbm, smem, smem, hbm, hbm, hbm, hbm, hbm],
        out_specs=(hbm, hbm),
        scratch_shapes=[
            pltpu.VMEM((wide, node_rows, width), bf16),
            pltpu.VMEM(tile_blocks.shape[2:], bf16),
            pltpu.VMEM((hidden_width, hidden_width), bf16),
            pltpu.VMEM((node_rows, hidden_width), bf16),
            pltpu.VMEM((width, hidden_width), bf16),
            pltpu.VMEM((width, hidden_width), bf16),
            pltpu.SMEM(tile_count.shape, jnp.int32),
            pltpu.VMEM((narrow, node_rows // side, side, wide * group), bf16),
            pltpu.VMEM((node_rows, hidden_width), f32),
            pltpu.VMEM((node_rows, hidden_width), f32),
            pltpu.VMEM((2, 2, group, hidden_width), bf16),
            pltpu.VMEM((2, 2, group, hidden_width), bf16),
            pltpu.VMEM((node_rows, hidden_width), bf16),
            pltpu.VMEM((node_rows, width), bf16),
            pltpu.VMEM((node_rows, hidden_width), bf16),
            pltpu.VMEM((node_rows, hidden_width), bf16),
            pltpu.VMEM((3, width, hidden_width), f32),
            pltpu.VMEM((3, width, hidden_width), bf16),
            pltpu.VMEM((z_size, 3, piece, hidden_width), bf16),
            pltpu.VMEM((z_size, 3, piece, hidden_width), bf16),
            pltpu.VMEM((z_size, 3, piece, hidden_width), bf16),
            pltpu.VMEM((3, width, hidden_width), bf16),
            pltpu.VMEM((node_rows, width), f32),
            pltpu.SemaphoreType.DMA((9,)),
            pltpu.SemaphoreType.DMA((copies,)),
            pltpu.SemaphoreType.DMA((copies,)),
        ],
        compiler_params=pltpu.CompilerParams(
            collective_id=0, has_side_effects=True, vmem_limit_bytes=63 * 1024 * 1024
        ),
    )(
        features, tile_blocks, tile_rows, tile_cols, tile_count,
        neighbor_weight, root_weight, output_weight, cotangent,
    )
    return pl.pallas_call(
        finish_kernel,
        out_shape=(
            jax.ShapeDtypeStruct((node_rows, width), bf16),
            jax.ShapeDtypeStruct((width, hidden_width), f32),
            jax.ShapeDtypeStruct((width, hidden_width), f32),
            jax.ShapeDtypeStruct((hidden_width, width), f32),
        ),
        in_specs=[hbm] * 3,
        out_specs=(hbm,) * 4,
        scratch_shapes=[
            pltpu.VMEM((node_rows, width), bf16),
            pltpu.VMEM((node_rows, width), f32),
            pltpu.VMEM((3, width, hidden_width), bf16),
            pltpu.VMEM((node_rows, width), bf16),
            pltpu.VMEM((width, hidden_width), f32),
            pltpu.VMEM((width, hidden_width), f32),
            pltpu.VMEM((hidden_width, width), f32),
            pltpu.SemaphoreType.DMA((5,)),
            pltpu.SemaphoreType.DMA((4,)),
        ],
        compiler_params=pltpu.CompilerParams(vmem_limit_bytes=63 * 1024 * 1024),
    )(features, product, grads)


def solution(mesh):
    wide, narrow = mesh.shape["wide"], mesh.shape["narrow"]
    if wide == 8 and narrow == 4:
        per_device = functools.partial(per_device_fused, wide, narrow)
    else:
        per_device = per_device_large
    return jax.shard_map(
        per_device,
        mesh=mesh,
        in_specs=(
            P("wide", "narrow"),
            P("wide", "narrow", None, None, None),
            P("wide", "narrow", None),
            P("wide", "narrow", None),
            P("wide", "narrow"),
            P("narrow", None),
            P("narrow", None),
            P(),
            P("wide", None),
        ),
        out_specs=(P("wide", "narrow"), P("narrow", None), P("narrow", None), P(None, "narrow")),
        check_vma=False,
    )
```

```python
import functools
import math

import jax
import jax.numpy as jnp
from jax import lax
from jax.experimental import pallas as pl
from jax.experimental.pallas import tpu as pltpu
from jax.sharding import PartitionSpec as P


def tile_sum(block_tiles, row_ids, col_ids, live_count, column_tiles, tile_rows_count):
    capacity = block_tiles.shape[0]
    block_size = math.gcd(capacity, 24)
    tile_side = block_tiles.shape[-1]
    feature_width = column_tiles.shape[-1]
    row_range = jnp.arange(tile_rows_count, dtype=jnp.int32)
    slot_range = jnp.arange(block_size, dtype=jnp.int32)

    def one_turn(turn_index, running):
        first_slot = turn_index * block_size
        some_tiles = lax.dynamic_slice_in_dim(block_tiles, first_slot, block_size, 0)
        some_rows = lax.dynamic_slice_in_dim(row_ids, first_slot, block_size, 0)
        some_cols = lax.dynamic_slice_in_dim(col_ids, first_slot, block_size, 0)
        picked = column_tiles[some_cols]
        product = jnp.einsum("tij,tjh->tih", some_tiles, picked, preferred_element_type=jnp.float32)
        alive = (first_slot + slot_range < live_count).astype(jnp.float32)
        placing = alive[:, None] * (some_rows[:, None] == row_range[None, :]).astype(jnp.float32)
        return running + jnp.einsum("tr,tih->rih", placing, product)

    block_turns = (live_count + block_size - 1) // block_size
    start_value = jnp.zeros((tile_rows_count, tile_side, feature_width), jnp.float32)
    summed = lax.fori_loop(0, block_turns, one_turn, start_value)
    return summed.reshape(tile_rows_count * tile_side, feature_width)


def per_device_large(
    features,
    tile_blocks,
    tile_rows,
    tile_cols,
    tile_count,
    neighbor_weight,
    root_weight,
    output_weight,
    cotangent,
):
    node_rows = features.shape[0]
    slice_width = features.shape[1]
    wide_count = lax.axis_size("wide")
    narrow_count = lax.axis_size("narrow")
    tile_side = tile_blocks.shape[-1]
    tile_rows_count = node_rows // tile_side
    group_rows = node_rows // narrow_count
    all_tiles, all_rows, all_cols, all_counts = (
        lax.all_gather(tile_blocks, "narrow", axis=1, tiled=True),
        lax.all_gather(tile_rows, "narrow", axis=1, tiled=True),
        lax.all_gather(tile_cols, "narrow", axis=1, tiled=True),
        lax.all_gather(tile_count, "narrow", axis=1, tiled=True),
    )
    columns = lax.all_gather(features, "wide", axis=0, tiled=True)
    groups = columns.reshape(wide_count, narrow_count, group_rows, slice_width).transpose(
        1, 0, 2, 3
    )
    groups = groups.reshape(narrow_count, -1, tile_side, slice_width)
    running = jnp.zeros((node_rows, slice_width), jnp.float32)
    for source in range(narrow_count):
        running = running + tile_sum(
            all_tiles[0, source],
            all_rows[0, source],
            all_cols[0, source],
            all_counts[0, source],
            groups[source],
            tile_rows_count,
        )
    agg = running.astype(jnp.bfloat16)
    partial_pre = jnp.dot(agg, neighbor_weight, preferred_element_type=jnp.float32) + jnp.dot(
        features, root_weight, preferred_element_type=jnp.float32
    )
    pre = lax.psum(partial_pre, "narrow")
    hidden = jax.nn.silu(pre).astype(jnp.bfloat16)
    narrow_index = lax.axis_index("narrow")
    out_columns = lax.dynamic_slice_in_dim(
        output_weight, narrow_index * slice_width, slice_width, 1
    )
    layer_output = (
        features.astype(jnp.float32)
        + jnp.dot(hidden, out_columns, preferred_element_type=jnp.float32)
    ).astype(jnp.bfloat16)
    hidden_grad = jnp.dot(cotangent, output_weight.T, preferred_element_type=jnp.float32)
    sigmoid_pre = jax.nn.sigmoid(pre)
    pre_grad = (hidden_grad * sigmoid_pre * (1.0 + pre * (1.0 - sigmoid_pre))).astype(jnp.bfloat16)
    cot_columns = lax.dynamic_slice_in_dim(cotangent, narrow_index * slice_width, slice_width, 1)
    neighbor_part = jnp.dot(agg.T, pre_grad, preferred_element_type=jnp.float32)
    root_part = jnp.dot(features.T, pre_grad, preferred_element_type=jnp.float32)
    output_part = jnp.dot(hidden.T, cot_columns, preferred_element_type=jnp.float32)
    neighbor_grad, root_grad, output_grad = lax.psum(
        (neighbor_part, root_part, output_part), "wide"
    )
    return (layer_output, neighbor_grad, root_grad, output_grad)


Y_SIZE = 2
CORES = 2
MESH = pl.DeviceIdType.MESH


def fused_kernel(
    wide, narrow,
    x_hbm, t_hbm, rows_ref, cols_ref, count_hbm, wn_hbm, wr_hbm, ow_hbm, cot_hbm,
    grads_out, lo_out,
    xf, tiles, ow, cot, wn, wr, count_ref, dense, part, hidden_grad, sent, came, pre_all, agg,
    pg, hid, grad32, grad, from_y, to_z, from_z, gall, lo,
    local_sem, send_sem, recv_sem,
):
    z_size = wide // Y_SIZE
    me_b = lax.axis_index("wide")
    me_n = lax.axis_index("narrow")
    z, y = me_b // Y_SIZE, me_b % Y_SIZE
    other_y = 1 - y
    core_n = me_n // CORES * CORES + (1 - me_n % CORES)
    x_n = (me_n + CORES) % narrow
    xc_n = (core_n + CORES) % narrow
    node_rows, width = x_hbm.shape
    hidden_width = ow_hbm.shape[0]
    group = node_rows // narrow
    side = t_hbm.shape[-1]
    slots = t_hbm.shape[2]
    piece = width // wide
    tile_rows_count = node_rows // side
    across = dense.shape[-1] // side
    f32, bf16 = jnp.float32, jnp.bfloat16
    y_dev = (z * Y_SIZE + other_y, me_n)

    def group_rows(n):
        return pl.ds(pl.multiple_of(n * group, group), group)

    def slice_cols(n):
        return pl.ds(pl.multiple_of(n * width, width), width)

    def z_at(dz):
        return lax.rem(z + dz, z_size)

    def z_dev(dz):
        return (z_at(dz) * Y_SIZE + y, me_n)

    def z_source(dz):
        return lax.rem(z + z_size - dz, z_size) * Y_SIZE + y

    used = [0]
    pending = []

    def send(src, dst, device):
        k = used[0]
        used[0] += 1
        copy = pltpu.make_async_remote_copy(
            src_ref=src, dst_ref=dst, send_sem=send_sem.at[k], recv_sem=recv_sem.at[k],
            device_id=device, device_id_type=MESH,
        )
        copy.start()
        pending.append(copy)
        return copy

    barrier = pltpu.get_barrier_semaphore()
    partners = [(me_b, n) for n in (core_n, x_n, xc_n)]
    partners += [z_dev(dz) for dz in range(1, z_size)] + [y_dev]
    for device in partners:
        pl.semaphore_signal(barrier, inc=1, device_id=device, device_id_type=MESH)

    local = [
        pltpu.make_async_copy(src, dst, local_sem.at[k])
        for k, (src, dst) in enumerate(
            (
                (count_hbm, count_ref),
                (t_hbm.at[0, 0], tiles),
                (x_hbm, xf.at[me_b]),
                (wr_hbm, wr),
                (wn_hbm, wn),
                (cot_hbm, cot),
                (ow_hbm, ow),
            )
        )
    ]
    for copy in local:
        copy.start()
    count_copy, tile_copy, x_copy, wr_copy, wn_copy, cot_copy, ow_copy = local

    count_copy.wait()
    live = count_ref[0, 0]
    chunk = 32
    positions = tile_rows_count * across
    steps = side // chunk

    def densify(step):
        at = pl.ds(step * chunk, chunk)

        def add_slot(s, sums):
            tile = tiles[s, at, :].astype(f32)
            place = rows_ref[0, 0, s] * across + cols_ref[0, 0, s]
            place = jnp.where(s < live, place, -1)
            return tuple(
                sums[p] + tile * jnp.where(place == p, 1.0, 0.0).astype(f32)
                for p in range(positions)
            )

        sums = lax.fori_loop(
            0, slots, add_slot,
            tuple(jnp.zeros((chunk, side), f32) for _ in range(positions)),
            unroll=4,
        )
        for p in range(positions):
            dense[me_n, p // across, at, pl.ds(p % across * side, side)] = sums[p].astype(bf16)

    def slab(n, step):
        return dense.at[n, :, pl.ds(step * chunk, chunk), :]

    pl.semaphore_wait(barrier, len(partners))
    z_order = sorted(range(1, z_size), key=lambda dz: abs(dz - z_size / 2))
    x_halves = [pl.ds(0, node_rows)]
    blocks = {
        (dz, h): send(x_hbm.at[x_halves[h]], xf.at[me_b, x_halves[h]], z_dev(dz))
        for h in range(1)
        for dz in z_order
    }
    y_blocks = [send(x_hbm, xf.at[me_b], y_dev)]
    tile_copy.wait()
    dense_x, dense_core, dense_fwd = [], [], []
    for step in range(steps):
        densify(step)
        dense_x.append(send(slab(me_n, step), slab(me_n, step), (me_b, x_n)))
        dense_core.append(send(slab(me_n, step), slab(me_n, step), (me_b, core_n)))

    def pass_block(dz, h):
        blocks[dz, h].wait_recv()
        part_of = xf.at[z_source(dz), x_halves[h]]
        y_blocks.append(send(part_of, part_of, y_dev))

    def pass_slab(step):
        dense_x[step].wait_recv()
        dense_fwd.append(send(slab(x_n, step), slab(x_n, step), (me_b, core_n)))

    for step in range(steps // 2):
        pass_slab(step)
    for dz in z_order[1:] + z_order[:1]:
        pass_block(dz, 0)
    for step in range(steps // 2, steps):
        pass_slab(step)
    x_copy.wait()
    wr_copy.wait()
    wn_copy.wait()
    part[...] = jnp.dot(xf[me_b], wr[...], preferred_element_type=f32)

    for copy in y_blocks:
        copy.wait_recv()

    def product(n):
        column_tiles = xf[:, group_rows(n), :].reshape(wide * group, width)
        return jnp.dot(
            dense[n].reshape(node_rows, wide * group), column_tiles, preferred_element_type=f32
        )

    total = product(me_n)
    for copy in dense_core:
        copy.wait_recv()
    total = total + product(core_n)
    total = total + product(x_n)
    for copy in dense_fwd:
        copy.wait_recv()
    total = total + product(xc_n)
    agg[...] = total.astype(bf16)

    def pre_rows(core, q):
        return pl.ds(pl.multiple_of(core * 2 * group + q * group, group), group)

    def gates(rows, pre):
        sig = jax.nn.sigmoid(pre)
        pg[rows, :] = (hidden_grad[rows, :] * sig * (1.0 + pre * (1.0 - sig))).astype(bf16)
        hid[rows, :] = (pre * sig).astype(bf16)

    def half_pre(core):
        rows = pl.ds(pl.multiple_of(core * 2 * group, group), 2 * group)
        return part[rows, :] + jnp.dot(agg[rows, :], wn[...], preferred_element_type=f32)

    my_core = me_n % CORES
    sent[0] = half_pre(1 - my_core).astype(bf16).reshape(2, group, hidden_width)
    to_core = [send(sent.at[0, q], came.at[0, q], (me_b, core_n)) for q in range(2)]
    kept = half_pre(my_core).reshape(2, group, hidden_width)
    kept = [kept[0], kept[1]]
    to_x, back = [], []
    for q in range(2):
        to_core[q].wait_recv()
        kept[q] = kept[q] + came[0, q].astype(f32)
        sent[1, q] = kept[q].astype(bf16)
        to_x.append(send(sent.at[1, q], came.at[1, q], (me_b, x_n)))
    cot_copy.wait()
    ow_copy.wait()
    hidden_grad[...] = lax.dot_general(
        cot[...], ow[...], (((1,), (1,)), ((), ())), preferred_element_type=f32
    )
    for q in range(2):
        to_x[q].wait_recv()
        pre = kept[q] + came[1, q].astype(f32)
        rows = pre_rows(my_core, q)
        pre_all[rows, :] = pre.astype(bf16)
        back.append(send(pre_all.at[rows, :], pre_all.at[rows, :], (me_b, core_n)))
        gates(rows, pre)
    for q in range(2):
        back[q].wait_recv()
        rows = pre_rows(1 - my_core, q)
        gates(rows, pre_all[rows, :].astype(f32))

    contract_rows = (((0,), (0,)), ((), ()))
    tracks = (pl.ds(0, 2), pl.ds(2, 1))

    def piece_of(track, b):
        return (tracks[track], pl.ds(pl.multiple_of(b * piece, piece), piece), slice(None))

    def fill(k, left, right):
        value = lax.dot_general(left, right, contract_rows, preferred_element_type=f32)
        grad32[k] = value
        grad[k] = value.astype(bf16)

    def to_other_y(track):
        return [
            send(
                grad.at[piece_of(track, z_at(dz) * Y_SIZE + other_y)],
                from_y.at[dz, tracks[track]],
                y_dev,
            )
            for dz in z_order + [0]
        ]

    halves = []
    operands = ((agg[...], pg[...]), (xf[me_b], pg[...]), (cot[:, slice_cols(me_n)], hid[...]))
    for k, (left, right) in enumerate(operands):
        fill(k, left, right)
        if k:
            halves.append(to_other_y(k - 1))

    sums, arriving_z = [], []
    for track in range(2):
        along = tracks[track]
        arriving_z.append([])
        for dz, copy in zip(z_order + [0], halves[track]):
            copy.wait_recv()
            both = grad32[piece_of(track, z_at(dz) * Y_SIZE + y)] + from_y[dz, along].astype(f32)
            if dz:
                to_z[dz, along] = both.astype(bf16)
                arriving_z[track].append(
                    (dz, send(to_z.at[dz, along], from_z.at[dz, along], z_dev(dz)))
                )
        sums.append(both)
    lo[...] = jnp.dot(hid[...], ow[:, slice_cols(me_n)], preferred_element_type=f32)
    lo_copy = pltpu.make_async_copy(lo, lo_out, local_sem.at[7])
    lo_copy.start()
    last, done = [], []
    for track in range(2):
        both = sums[track]
        for dz, copy in arriving_z[track]:
            copy.wait_recv()
            both = both + from_z[dz, tracks[track]].astype(f32)
        own = piece_of(track, me_b)
        gall[own] = both.astype(bf16)
        done.append({dz: send(gall.at[own], gall.at[own], z_dev(dz)) for dz in z_order})
        last.append(send(gall.at[own], gall.at[own], y_dev))
    for track in range(2):
        for dz in z_order[1:] + z_order[:1]:
            done[track][dz].wait_recv()
            at = piece_of(track, z_source(dz))
            last.append(send(gall.at[at], gall.at[at], y_dev))
    for copy in last:
        copy.wait_recv()
    out_copy = pltpu.make_async_copy(gall, grads_out, local_sem.at[8])
    out_copy.start()
    for copy in pending:
        copy.wait_send()
    lo_copy.wait()
    out_copy.wait()


def finish_kernel(
    x_hbm, product_hbm, grads_hbm, out_hbm, neighbor_hbm, root_hbm, output_hbm,
    x, product, grads, out, neighbor, root, output, in_sem, out_sem,
):
    f32 = jnp.float32
    pairs = [(grads_hbm.at[k], grads.at[k]) for k in (2, 0, 1)]
    pairs += [(x_hbm, x), (product_hbm, product)]
    arriving = [
        pltpu.make_async_copy(src, dst, in_sem.at[k]) for k, (src, dst) in enumerate(pairs)
    ]
    for copy in arriving:
        copy.start()
    leaving = [
        pltpu.make_async_copy(src, dst, out_sem.at[k])
        for k, (src, dst) in enumerate(
            ((output, output_hbm), (neighbor, neighbor_hbm), (root, root_hbm), (out, out_hbm))
        )
    ]
    arriving[0].wait()
    output[...] = grads[2].astype(f32).T
    leaving[0].start()
    arriving[1].wait()
    neighbor[...] = grads[0].astype(f32)
    leaving[1].start()
    arriving[2].wait()
    root[...] = grads[1].astype(f32)
    leaving[2].start()
    arriving[3].wait()
    arriving[4].wait()
    out[...] = (x[...].astype(f32) + product[...]).astype(out.dtype)
    leaving[3].start()
    for copy in leaving:
        copy.wait()


def per_device_fused(
    wide, narrow,
    features, tile_blocks, tile_rows, tile_cols, tile_count,
    neighbor_weight, root_weight, output_weight, cotangent,
):
    node_rows, width = features.shape
    hidden_width = output_weight.shape[0]
    group = node_rows // narrow
    side = tile_blocks.shape[-1]
    z_size = wide // Y_SIZE
    piece = width // wide
    bf16, f32 = jnp.bfloat16, jnp.float32
    copies = 96
    hbm = pl.BlockSpec(memory_space=pltpu.HBM)
    smem = pl.BlockSpec(memory_space=pltpu.SMEM)
    grads, product = pl.pallas_call(
        functools.partial(fused_kernel, wide, narrow),
        out_shape=(
            jax.ShapeDtypeStruct((3, width, hidden_width), bf16),
            jax.ShapeDtypeStruct((node_rows, width), f32),
        ),
        in_specs=[hbm, hbm, smem, smem, hbm, hbm, hbm, hbm, hbm],
        out_specs=(hbm, hbm),
        scratch_shapes=[
            pltpu.VMEM((wide, node_rows, width), bf16),
            pltpu.VMEM(tile_blocks.shape[2:], bf16),
            pltpu.VMEM((hidden_width, hidden_width), bf16),
            pltpu.VMEM((node_rows, hidden_width), bf16),
            pltpu.VMEM((width, hidden_width), bf16),
            pltpu.VMEM((width, hidden_width), bf16),
            pltpu.SMEM(tile_count.shape, jnp.int32),
            pltpu.VMEM((narrow, node_rows // side, side, wide * group), bf16),
            pltpu.VMEM((node_rows, hidden_width), f32),
            pltpu.VMEM((node_rows, hidden_width), f32),
            pltpu.VMEM((2, 2, group, hidden_width), bf16),
            pltpu.VMEM((2, 2, group, hidden_width), bf16),
            pltpu.VMEM((node_rows, hidden_width), bf16),
            pltpu.VMEM((node_rows, width), bf16),
            pltpu.VMEM((node_rows, hidden_width), bf16),
            pltpu.VMEM((node_rows, hidden_width), bf16),
            pltpu.VMEM((3, width, hidden_width), f32),
            pltpu.VMEM((3, width, hidden_width), bf16),
            pltpu.VMEM((z_size, 3, piece, hidden_width), bf16),
            pltpu.VMEM((z_size, 3, piece, hidden_width), bf16),
            pltpu.VMEM((z_size, 3, piece, hidden_width), bf16),
            pltpu.VMEM((3, width, hidden_width), bf16),
            pltpu.VMEM((node_rows, width), f32),
            pltpu.SemaphoreType.DMA((9,)),
            pltpu.SemaphoreType.DMA((copies,)),
            pltpu.SemaphoreType.DMA((copies,)),
        ],
        compiler_params=pltpu.CompilerParams(
            collective_id=0, has_side_effects=True, vmem_limit_bytes=63 * 1024 * 1024
        ),
    )(
        features, tile_blocks, tile_rows, tile_cols, tile_count,
        neighbor_weight, root_weight, output_weight, cotangent,
    )
    return pl.pallas_call(
        finish_kernel,
        out_shape=(
            jax.ShapeDtypeStruct((node_rows, width), bf16),
            jax.ShapeDtypeStruct((width, hidden_width), f32),
            jax.ShapeDtypeStruct((width, hidden_width), f32),
            jax.ShapeDtypeStruct((hidden_width, width), f32),
        ),
        in_specs=[hbm] * 3,
        out_specs=(hbm,) * 4,
        scratch_shapes=[
            pltpu.VMEM((node_rows, width), bf16),
            pltpu.VMEM((node_rows, width), f32),
            pltpu.VMEM((3, width, hidden_width), bf16),
            pltpu.VMEM((node_rows, width), bf16),
            pltpu.VMEM((width, hidden_width), f32),
            pltpu.VMEM((width, hidden_width), f32),
            pltpu.VMEM((hidden_width, width), f32),
            pltpu.SemaphoreType.DMA((5,)),
            pltpu.SemaphoreType.DMA((4,)),
        ],
        compiler_params=pltpu.CompilerParams(vmem_limit_bytes=63 * 1024 * 1024),
    )(features, product, grads)


def solution(mesh):
    wide, narrow = mesh.shape["wide"], mesh.shape["narrow"]
    if wide == 8 and narrow == 4:
        per_device = functools.partial(per_device_fused, wide, narrow)
    else:
        per_device = per_device_large
    return jax.shard_map(
        per_device,
        mesh=mesh,
        in_specs=(
            P("wide", "narrow"),
            P("wide", "narrow", None, None, None),
            P("wide", "narrow", None),
            P("wide", "narrow", None),
            P("wide", "narrow"),
            P("narrow", None),
            P("narrow", None),
            P(),
            P("wide", None),
        ),
        out_specs=(P("wide", "narrow"), P("narrow", None), P("narrow", None), P(None, "narrow")),
        check_vma=False,
    )
```
